32 devices in a mesh: wide: 16 (over z, y, x), narrow: 2 (over core).
Axes of the slice: x: 2, y: 2, z: 4, core: 2. Of those that a mesh axis runs over, the one named last changes fastest.
Arguments:
- tokens: bfloat16 [16384, 768], P(('wide', 'narrow')), may hold values from -6 to 6
- segment: int32 [16384], P(('wide', 'narrow')), may hold values from 0 to 3, as said below
- cotangent: bfloat16 [16384, 768], P(('wide', 'narrow')), may hold values from -6 to 6
- w_up: bfloat16 [768, 3072], P(('wide', 'narrow')), may hold values from -0.21875 to 0.21875
- w_value: bfloat16 [768, 1536], P(('wide', 'narrow')), may hold values from -0.21875 to 0.21875
- w_proj: bfloat16 [3072, 1536], P(('wide', 'narrow')), may hold values from -0.109375 to 0.109375
- w_out: bfloat16 [1536, 768], P(('wide', 'narrow')), may hold values from -0.3125 to 0.3125
- norm_gain: bfloat16 [768], P(('wide', 'narrow')), may hold values from 0.5 to 1.5
- norm_bias: bfloat16 [768], P(('wide', 'narrow')), may hold values from -3 to 3
- bias_up: bfloat16 [3072], P(('wide', 'narrow')), may hold values from -3 to 3
- bias_value: bfloat16 [1536], P(('wide', 'narrow')), may hold values from -3 to 3
- bias_proj: bfloat16 [1536], P(('wide', 'narrow')), may hold values from -3 to 3
- bias_out: bfloat16 [768], P(('wide', 'narrow')), may hold values from -3 to 3
- log_rate: bfloat16 [1536, 64], P(('wide', 'narrow')), may hold values from -1 to 1
- log_step: bfloat16 [1536], P(('wide', 'narrow')), may hold values from -7 to -2.5
- input_map: bfloat16 [1536, 64], P(('wide', 'narrow')), may hold values from -3 to 3
- output_map: bfloat16 [1536, 64], P(('wide', 'narrow')), may hold values from -3 to 3
- skip_gain: bfloat16 [1536], P(('wide', 'narrow')), may hold values from -4 to 4
Outputs:
- result: bfloat16 [16384, 768], P(('wide', 'narrow'))
- grad_tokens: float32 [16384, 768], P(('wide', 'narrow'))
- grad_w_up: float32 [768, 3072], P(('wide', 'narrow'))
- grad_w_value: float32 [768, 1536], P(('wide', 'narrow'))
- grad_w_proj: float32 [3072, 1536], P(('wide', 'narrow'))
- grad_w_out: float32 [1536, 768], P(('wide', 'narrow'))
- grad_norm_gain: float32 [768], P(('wide', 'narrow'))
- grad_norm_bias: float32 [768], P(('wide', 'narrow'))
- grad_bias_up: float32 [3072], P(('wide', 'narrow'))
- grad_bias_value: float32 [1536], P(('wide', 'narrow'))
- grad_bias_proj: float32 [1536], P(('wide', 'narrow'))
- grad_bias_out: float32 [768], P(('wide', 'narrow'))
- grad_log_rate: float32 [1536, 64], P(('wide', 'narrow'))
- grad_log_step: float32 [1536], P(('wide', 'narrow'))
- grad_input_map: float32 [1536, 64], P(('wide', 'narrow'))
- grad_output_map: float32 [1536, 64], P(('wide', 'narrow'))
- grad_skip_gain: float32 [1536], P(('wide', 'narrow'))
The draws below stay inside these ranges and needn't reach their ends.
Inputs may be any that keep to these rules, and one draw needn't show every extreme that they name: Within each device's block of 512 tokens, segment numbers whole sequences from 0 upward: first some sequences of 512 tokens, then sequences of 128 tokens; some device holds only short ones.
All inputs are finite; a program needn't handle non-finite values.
Results may differ from the reference program's by a relative error of at most 0.007.
Values may be sent and summed in bfloat16 or wider, within the bound.
No kernel may reach another device: no remote copies, remote signals or barrier semaphores. Data moves between devices by JAX's collectives and lax.ppermute only.
A program may use at most 384 MiB of HBM per device.

```python
import jax
import jax.numpy as jnp
from jax import lax

D = 768
FF = 3072
S = 1536
N = 64
TOK_DEV = 512
LONG = 512
SHORT = 128
BLOCK = 32
TOKENS = 16384
N_WIDE = 16
N_NARROW = 2


def draw_segment(key, part):
    key = jax.random.fold_in(key, 11)
    devices = TOKENS // TOK_DEV
    longs = jax.random.randint(key, (devices,), 0, TOK_DEV // LONG + 1)
    chosen = jax.random.randint(jax.random.fold_in(key, 1), (), 0, devices)
    longs = jnp.where(jnp.arange(devices) == chosen, 0, longs)
    places = jnp.arange(TOK_DEV)[None, :]
    border = longs[:, None] * LONG
    labels = jnp.where(places < border, places // LONG, longs[:, None] + (places - border) // SHORT)
    return labels.reshape(TOKENS).astype(jnp.int32)


def block_scale(key, dims, cuts, least, top_value):
    def one(dim, blocks):
        draws = jax.random.uniform(jax.random.fold_in(jax.random.fold_in(key, 6), dim), (blocks,), jnp.float32, least / len(cuts), top_value / len(cuts))
        return jnp.repeat(jnp.exp(draws), dims[dim] // blocks).reshape((-1,) + (1,) * (len(dims) - dim - 1))

    factor_of = one(*cuts[0])
    for cut in cuts[1:]:
        factor_of = factor_of * one(*cut)
    return factor_of


def normal_values(rng, shape, scale, reach, shards=(), held_as=jnp.bfloat16):
    values = jax.random.normal(rng, shape, jnp.float32) * scale
    if len(shards) > 0:
        values = block_scale(rng, shape, shards, -0.22, 0.18) * values
    return jnp.clip(values, min=-reach, max=reach).astype(held_as)


def setup_inputs(seed: int = 0) -> dict:
    arg_keys = jax.random.split(jax.random.key(seed), 19)
    tokens = normal_values(arg_keys[0], (TOKENS, D), 1.0, 6.0, ((0, 32),))
    segment = draw_segment(jax.random.fold_in(arg_keys[18], 71), 0)
    cotangent = normal_values(arg_keys[2], (TOKENS, D), 1.0, 6.0, ((0, 32),))
    w_up = normal_values(arg_keys[3], (D, FF), D ** -0.5, 0.21875, ((0, 32),))
    w_value = normal_values(arg_keys[4], (D, S), D ** -0.5, 0.21875, ((0, 32),))
    w_proj = normal_values(arg_keys[5], (FF, S), FF ** -0.5, 0.109375, ((0, 32),))
    w_out = normal_values(arg_keys[6], (S, D), (S // 4) ** -0.5, 0.3125, ((0, 32),))
    norm_gain = jnp.clip(1.0 + 0.1 * jax.random.normal(arg_keys[7], (D,), jnp.float32), 0.5, 1.5).astype(jnp.bfloat16)
    norm_bias = normal_values(arg_keys[8], (D,), 0.3, 3.0, ((0, 32),))
    bias_up = normal_values(arg_keys[9], (FF,), 0.3, 3.0, ((0, 32),))
    bias_value = normal_values(arg_keys[10], (S,), 0.3, 3.0, ((0, 32),))
    bias_proj = normal_values(arg_keys[11], (S,), 0.3, 3.0, ((0, 32),))
    bias_out = normal_values(arg_keys[12], (D,), 0.3, 3.0, ((0, 32),))
    log_rate = jnp.clip(jax.random.uniform(arg_keys[13], (S, N), jnp.float32, -1.0, 1.0) * block_scale(arg_keys[13], (S, N), ((0, 32),), -0.4, 0.0), -1.0, 1.0).astype(jnp.bfloat16)
    log_step = jnp.clip(-7.0 + 4.5 * jax.random.uniform(arg_keys[14], (S,), jnp.float32) ** block_scale(arg_keys[14], (S,), ((0, 32),), -0.2, 0.2), -7.0, -2.5).astype(jnp.bfloat16)
    input_map = normal_values(arg_keys[15], (S, N), 0.5, 3.0, ((0, 32),))
    output_map = normal_values(arg_keys[16], (S, N), 0.5, 3.0, ((0, 32),))
    skip_gain = normal_values(arg_keys[17], (S,), 1.0, 4.0, ((0, 32),))
    return {"tokens": tokens, "segment": segment, "cotangent": cotangent, "w_up": w_up, "w_value": w_value, "w_proj": w_proj, "w_out": w_out, "norm_gain": norm_gain, "norm_bias": norm_bias, "bias_up": bias_up, "bias_value": bias_value, "bias_proj": bias_proj, "bias_out": bias_out, "log_rate": log_rate, "log_step": log_step, "input_map": input_map, "output_map": output_map, "skip_gain": skip_gain}


@jax.custom_vjp
def low(v):
    return lax.optimization_barrier(v.astype(jnp.bfloat16)).astype(jnp.float32)

@jax.custom_vjp
def low_back(v):
    return v

def low_keep(v):
    return (low(v), None)

def low_pass(kept, grad):
    return (grad,)

def back_keep(v):
    return (v, None)

def back_low(kept, grad):
    return (low(grad),)
low.defvjp(low_keep, low_pass)
low_back.defvjp(back_keep, back_low)

def matmul(left, right):
    return jnp.dot(left, right, precision=lax.Precision.HIGHEST, preferred_element_type=jnp.float32)

def ssm_half(values, labels, log_rate, log_step, input_map, output_map):
    length, width = values.shape
    count = length // BLOCK
    rate = -jnp.exp(log_rate)
    step_size = jnp.exp(log_step)[:, None]
    decay_log = (step_size * rate).T
    factor = jnp.exp(decay_log)
    weight = (output_map * (jnp.exp(step_size * rate) - 1.0) / rate * input_map).T
    lags = jnp.arange(BLOCK, dtype=jnp.float32)
    powers = jnp.exp(lags[:, None, None] * decay_log[None])
    kernel = jnp.einsum('lnh,nh->lh', powers, weight, precision=lax.Precision.HIGHEST)
    places = jnp.arange(BLOCK)
    onehot = (places[:, None, None] - places[None, :, None] == places[None, None, :]).astype(jnp.float32)
    toeplitz = jnp.einsum('tsl,lh->tsh', onehot, kernel, precision=lax.Precision.HIGHEST)
    blocks = values.reshape(count, BLOCK, width)
    inner = jnp.einsum('tsh,bsh->bth', toeplitz, blocks, precision=lax.Precision.HIGHEST)
    ends = jnp.einsum('snh,bsh->bnh', powers[::-1], blocks, precision=lax.Precision.HIGHEST)
    heads = labels.reshape(count, BLOCK)
    carry_on = jnp.concatenate([jnp.zeros((1,), jnp.float32), (heads[1:, 0] == heads[:-1, -1]).astype(jnp.float32)])
    full_decay = jnp.exp(BLOCK * decay_log)

    def advance(state, item):
        flag, local = item
        entering = flag * state
        return (full_decay * entering + local, entering)
    start = jnp.zeros(decay_log.shape, jnp.float32)
    finals, entering = lax.scan(advance, start, (carry_on, ends))
    lead = powers * factor[None] * weight[None]
    outer = jnp.einsum('tnh,bnh->bth', lead, entering, precision=lax.Precision.HIGHEST)
    return (inner + outer).reshape(length, width)

def mixer(values, labels, log_rate, log_step, input_map, output_map, skip_gain):
    half = values.shape[1] // 2
    forward_part = ssm_half(values[:, :half], labels, log_rate[:half], log_step[:half], input_map[:half], output_map[:half])
    backward_part = ssm_half(values[::-1, half:], labels[::-1], log_rate[half:], log_step[half:], input_map[half:], output_map[half:])[::-1]
    return jnp.concatenate([forward_part, backward_part], axis=1) + skip_gain * values

def layer(inputs, labels, group_rows, w_up, w_value, w_proj, w_out, norm_gain, norm_bias, bias_up, bias_value, bias_proj, bias_out, log_rate, log_step, input_map, output_map, skip_gain):
    average = lax.optimization_barrier(jnp.mean(inputs, axis=-1, keepdims=True))
    centred = inputs - average
    spread = lax.optimization_barrier(jnp.mean(centred * centred, axis=-1, keepdims=True))
    normed = centred * lax.rsqrt(spread + 1e-05) * norm_gain + norm_bias
    normed_low = low(normed)
    up_pre = low_back(matmul(normed_low, w_up) + bias_up)
    up_low = low(jax.nn.gelu(up_pre))
    value_pre = low_back(matmul(normed_low, w_value) + bias_value)
    value_act = jax.nn.gelu(value_pre)

    def one_device(pair):
        return mixer(pair[0], pair[1], log_rate, log_step, input_map, output_map, skip_gain)
    mixed = lax.map(jax.checkpoint(one_device), (value_act.reshape(group_rows, TOK_DEV, S), labels.reshape(group_rows, TOK_DEV)))
    mixed = mixed.reshape(group_rows * TOK_DEV, S)
    proj = low_back(matmul(up_low, w_proj) + bias_proj)
    gated_low = low(mixed * proj)
    return inputs + matmul(gated_low, w_out) + bias_out

def reference(tokens, segment, cotangent, w_up, w_value, w_proj, w_out, norm_gain, norm_bias, bias_up, bias_value, bias_proj, bias_out, log_rate, log_step, input_map, output_map, skip_gain):
    params = tuple((p.astype(jnp.float32) for p in (w_up, w_value, w_proj, w_out, norm_gain, norm_bias, bias_up, bias_value, bias_proj, bias_out, log_rate, log_step, input_map, output_map, skip_gain)))
    devices = N_WIDE * N_NARROW
    group_rows = 1
    for candidate in range(1, devices + 1):
        if devices % candidate == 0 and candidate * TOK_DEV <= 4096:
            group_rows = candidate
    groups = devices // group_rows
    extent = group_rows * TOK_DEV
    stacked = (tokens.astype(jnp.float32).reshape(groups, extent, D), segment.reshape(groups, extent), cotangent.astype(jnp.float32).reshape(groups, extent, D))

    def visit(totals, item):
        inputs, labels, upstream = item

        def apply(inputs_in, *weights):
            return layer(inputs_in, labels, group_rows, *weights)
        output, pullback = jax.vjp(apply, inputs, *params)
        grads = pullback(upstream)
        totals = tuple((a + b for a, b in zip(totals, grads[1:])))
        return (totals, (output.astype(jnp.bfloat16), grads[0]))
    zeros = tuple((jnp.zeros_like(p) for p in params))
    totals, (outputs, input_grads) = lax.scan(visit, zeros, stacked)
    return (outputs.reshape(TOKENS, D), input_grads.reshape(TOKENS, D), totals[0], totals[1], totals[2], totals[3], totals[4], totals[5], totals[6], totals[7], totals[8], totals[9], totals[10], totals[11], totals[12], totals[13], totals[14])
```

```python
import functools

import jax
import jax.numpy as jnp
from jax import lax
from jax.experimental import pallas as pl
from jax.experimental.pallas import tpu as pltpu
from jax.sharding import PartitionSpec as P

T = 32
NB = 32
f32, bf16 = jnp.float32, jnp.bfloat16

def iota(shape, dim): return lax.broadcasted_iota(jnp.int32, shape, dim)

def take(x, index, axis):
    return jnp.take_along_axis(x, index, axis=axis, mode="promise_in_bounds")

def turn(x, sign):
    row, lane = iota((8, 128), 0), iota((8, 128), 1)
    return take(x, (lane - sign * 32 * (row & 3)) & 127, 1)

def skew(x):
    row, chunk = iota((8, 128), 0), iota((8, 128), 1) >> 5
    return take(x, (row & 4) | ((chunk - row) & 3), 0)

def swap_chunks(x):
    return turn(skew(turn(x, 1)), -1)

def to_blocks(x):
    z = [swap_chunks(x[:, 128 * j:128 * j + 128]) for j in range(8)]
    low = iota((8, 128), 0) < 4
    left = [jnp.where(low, z[2 * i], pltpu.roll(z[2 * i + 1], 4, 0)) for i in range(4)]
    right = [jnp.where(low, pltpu.roll(z[2 * i], 4, 0), z[2 * i + 1]) for i in range(4)]
    return jnp.concatenate([jnp.concatenate(left, 0), jnp.concatenate(right, 0)], 1)

def from_blocks(y):
    low = iota((8, 128), 0) < 4
    out = []
    for i in range(4):
        l, r = y[8 * i:8 * i + 8, :128], y[8 * i:8 * i + 8, 128:]
        for z in (jnp.where(low, l, pltpu.roll(r, 4, 0)), jnp.where(low, pltpu.roll(l, 4, 0), r)):
            out.append(swap_chunks(z))
    return jnp.concatenate(out, 1)

def diagonal(y, half):
    part = y[:, 128 * half:128 * half + 128]
    chunk = iota(part.shape, 1) >> 5
    return jnp.concatenate([jnp.where(chunk == c, part, jnp.zeros_like(part)) for c in range(4)], 0)

def dot(a, b, dims=((1,), (0,))):
    return lax.dot_general(a, b, (dims, ((), ())), preferred_element_type=f32)

def two(parts): return jnp.concatenate(parts, 1)

def shift(x, k, back):
    n = 128 - k if back else k
    return two([pltpu.roll(x[:, :128], n, 1), pltpu.roll(x[:, 128:], n, 1)])

def spread(x3):
    r = ((iota((24, 256), 0) & 7) == (iota((24, 256), 1) >> 5)).astype(f32).astype(bf16)
    return dot(x3, r, ((0,), (0,)))

def roll_halves(x, amount, **kw):
    return two([pltpu.roll(x[:, :128], amount, 1, **kw), pltpu.roll(x[:, 128:], amount, 1, **kw)])

def lag_rows(row, amount):
    row = roll_halves(jnp.broadcast_to(row, (8, 256)), amount)
    return roll_halves(jnp.concatenate([row] * 4, 0), 0, stride=1, stride_axis=0)

def gelu_parts(x):
    k = 0.7978845608028654
    t = jnp.tanh(k * (x + 0.044715 * (x * x * x)))
    return t, k

def gelu(x):
    t, k = gelu_parts(x)
    return 0.5 * x * (1.0 + t)

def gelu_grad(x):
    t, k = gelu_parts(x)
    return 0.5 * (1.0 + t) + 0.5 * x * (1.0 - t * t) * k * (1.0 + 3 * 0.044715 * x * x)

def halved(x):
    hi = x.astype(bf16)
    return hi, (x - hi.astype(f32)).astype(bf16)

def each(f, *lists):
    return [f(*items) for items in zip(*lists)]

def scans(es, fs, mask_ref, first, back):
    for i in range(4):
        moved = each(lambda e: shift(e, 1 << i, back), es)
        m = mask_ref[first + i:first + i + 1, :]
        es = each(lambda e, f, s: e + (f * m) * s, es, fs, moved)
        if i < 3: fs = each(lambda f: f * f, fs)
    return es

def halves_dot(lhs, rights, width):
    return two([dot(lhs[:, width * h:width * h + width], rights[h]) for h in range(2)])

def fwd_groups(rev, xs, d3s, w3s, drows, wrows, skips, masks):
    vs = each(gelu, xs)
    vys = each(lambda v: to_blocks(v).astype(bf16), vs)
    d1s, w1s = each(spread, d3s), each(spread, w3s)
    pos = iota((64, 256), 1) & 31
    p = (pos if rev else 31 - pos).astype(f32)
    pts = each(lambda d1: jnp.exp(p * d1), d1s)
    krows = each(lambda w1, pt: jnp.sum(w1 * pt, axis=0, keepdims=True), w1s, pts)
    row, lane = iota((T, 256), 0), iota((T, 256), 1) & 31
    valid = (lane >= row if rev else row >= lane)
    toeps = each(lambda k: jnp.where(valid, lag_rows(k, 0 if rev else 97), 0.0), krows)
    lhss = each(lambda pt, t: jnp.concatenate([pt, t], 0).astype(bf16), pts, toeps)
    boths = each(lambda lhs, vy: halves_dot(lhs, [diagonal(vy, h) for h in range(2)], 128), lhss, vys)
    fs = each(lambda d1: jnp.exp(float(T) * d1), d1s)
    hs = scans([b[:64] for b in boths], fs, masks, 0, rev)
    hes = each(lambda h: masks[0:1, :] * shift(h, 1, rev), hs)
    col = iota((T, 512), 0)
    q = (T - col if rev else col + 1).astype(f32)
    leads = each(lambda wrow, drow: (wrow * jnp.exp(q * drow)).astype(bf16), wrows, drows)
    outers = each(lambda lead, he: halves_dot(lead, [diagonal(he.astype(bf16), h) for h in range(2)], 256), leads, hes)
    return each(lambda b, o, skip, v: from_blocks(b[64:] + o) + skip * v, boths, outers, skips, vs), hes

def fwd_kernel(groups, unroll, dir_ref, x_ref, d3_ref, w3_ref, drow_ref, wrow_ref, skip_ref, mask_ref, out_ref, enter_ref):
    def body(rev, i, _):
        gs = [i * unroll + u for u in range(unroll)]
        rows = [pl.ds(pl.multiple_of(g * 8, 8), 8) for g in gs]
        pick = lambda ref, at: [ref[a] for a in at]
        pickr = lambda ref: [ref[r, :] for r in rows]
        pickf = lambda ref: [ref[pl.ds(g, 1), :] for g in gs]
        outs, enters = fwd_groups(rev, pickr(x_ref), pick(d3_ref, gs), pick(w3_ref, gs), pickf(drow_ref), pickf(wrow_ref), pickr(skip_ref), mask_ref)
        for g, r, o, e in zip(gs, rows, outs, enters):
            out_ref[r, :] = o
            enter_ref[g] = e
        return 0
    for rev in (False, True):
        @pl.when(dir_ref[0] == int(rev))
        def _(rev=rev):
            lax.fori_loop(0, groups // unroll, functools.partial(body, rev), 0)

def flip_rows(y):
    row = iota((8, 128), 0)
    tiles = [[take(y[8 * i : 8 * i + 8, 128 * h : 128 * h + 128], 7 - row, 0) for h in range(2)] for i in (3, 2, 1, 0)]
    return jnp.concatenate([two(t) for t in tiles], 0)

def bwd_groups(rev, at_group, xs, gms, hes, d3s, w3s, drows, skips, masks):
    vs = each(gelu, xs)
    vys = each(lambda v: to_blocks(v).astype(bf16), vs)
    gfs = each(to_blocks, gms)
    gys = each(lambda g: g.astype(bf16), gfs)
    gyrs = each(lambda g: flip_rows(g).astype(bf16), gfs)
    d1s, w1s = each(spread, d3s), each(spread, w3s)
    pos = iota((64, 256), 1) & 31
    p = (pos if rev else 31 - pos).astype(f32)
    pts = each(lambda d1: jnp.exp(p * d1), d1s)
    ppts = each(lambda pt: p * pt, pts)
    rs = each(lambda d1: jnp.exp((31.0 - p) * d1), d1s)
    ats = each(lambda r, d1: r * jnp.exp(d1), rs, d1s)
    apts = each(lambda at: (32.0 - p) * at, ats)
    krows = each(lambda w1, r: jnp.sum(w1 * r, axis=0, keepdims=True), w1s, rs)
    row, lane = iota((T, 256), 0), iota((T, 256), 1) & 31
    ok2 = (row >= lane if rev else lane >= row)
    toeps = each(lambda k: jnp.where(ok2, lag_rows(k, 97 if rev else 0), 0.0), krows)
    lhs_v = each(lambda ppt: ppt.astype(bf16), ppts)
    lhs_g = each(lambda at, apt, t: jnp.concatenate([at, apt, t], 0).astype(bf16), ats, apts, toeps)
    bdvs = each(lambda vy: [diagonal(vy, h) for h in range(2)], vys)
    bdgs = each(lambda gy: [diagonal(gy, h) for h in range(2)], gys)
    ees = each(lambda l, b: halves_dot(l, b, 128), lhs_v, bdvs)
    qqs = each(lambda l, b: halves_dot(l, b, 128), lhs_g, bdgs)
    ms = each(lambda gy, b: two([dot(gy[:, 128 * h:128 * h + 128], b[h], ((1,), (1,))) for h in range(2)]), gyrs, bdvs)
    fs = each(lambda d1: jnp.exp(float(T) * d1), d1s)
    n = len(xs)
    downs = scans(each(lambda w1, q: w1 * q[:64], w1s, qqs), fs, masks, 4, not rev)
    des = each(lambda h: masks[4:5, :] * shift(h, 1, not rev), downs)
    col = iota((T, 512), 0)
    pw = (col if rev else 31 - col).astype(f32)
    p2s = each(lambda drow: jnp.exp(pw * drow).astype(bf16), drows)
    dvs = each(lambda qq, p2, de: qq[128:] + halves_dot(p2, [diagonal(de.astype(bf16), h) for h in range(2)], 256), qqs, p2s, des)
    ok = (lane + row >= 31 if rev else lane + row <= 31)
    ms = each(lambda m: roll_halves(jnp.where(ok, m, 0.0), 0, stride=1, stride_axis=0), ms)
    dks = each(lambda m: jnp.sum(m, axis=0, keepdims=True), ms)
    if rev: dks = each(lambda dk: roll_halves(jnp.broadcast_to(dk, (8, 256)), 97)[:1], dks)
    zws = each(lambda he, qq, pt, dk: he * qq[:64] + pt * dk, hes, qqs, pts, dks)
    zds = each(lambda w1, he, qq, ppt, dk, de, ee, f: w1 * (he * qq[64:128] + ppt * dk) + de * (ee + float(T) * f * he), w1s, hes, qqs, ppts, dks, des, ees, fs)
    total = 0.0
    for u, (zw, zd) in enumerate(zip(zws, zds)):
        column = 8 * (at_group + u) + (iota((256, 128), 0) >> 5)
        ones = (iota((256, 128), 1) == column).astype(f32).astype(bf16)
        both = dot(jnp.concatenate([*halved(zw), *halved(zd)], 0), ones)
        total = total + jnp.concatenate([both[:64] + both[64:128], both[128:192] + both[192:]], 0)
    dvals = each(lambda dv, skip, gm, x: (from_blocks(dv) + skip * gm) * gelu_grad(x), dvs, skips, gms, xs)
    dskips = each(lambda gm, v: jnp.sum(gm * v, axis=1, keepdims=True), gms, vs)
    return dvals, total, dskips

def bwd_kernel(groups, unroll, dir_ref, x_ref, gm_ref, enter_ref, d3_ref, w3_ref, drow_ref, skip_ref, mask_ref, gv_ref, grads_ref, dskip_ref, dbias_ref):
    grads_ref[...] = jnp.zeros_like(grads_ref)
    def body(rev, i, _):
        gs = [i * unroll + u for u in range(unroll)]
        rows = [pl.ds(pl.multiple_of(g * 8, 8), 8) for g in gs]
        pick = lambda ref: [ref[a] for a in gs]
        pickr = lambda ref: [ref[r, :] for r in rows]
        pickf = lambda ref: [ref[pl.ds(g, 1), :] for g in gs]
        gms = pickr(gm_ref)
        dvals, total, dskips = bwd_groups(rev, i * unroll, pickr(x_ref), gms, pick(enter_ref), pick(d3_ref), pick(w3_ref), pickf(drow_ref), pickr(skip_ref), mask_ref)
        grads_ref[...] += total
        for r, a, c in zip(rows, dvals, dskips):
            dskip_ref[r, :] = c
            dbias_ref[r, :] = jnp.sum(a.astype(bf16).astype(f32), axis=1, keepdims=True)
        for u in range(0, unroll, 2):
            gv_ref[pl.ds(pl.multiple_of((i * unroll + u) * 8, 16), 16), :] = jnp.concatenate(dvals[u : u + 2], 0).astype(bf16)
        return 0
    for rev in (False, True):
        @pl.when(dir_ref[0] == int(rev))
        def _(rev=rev):
            lax.fori_loop(0, groups // unroll, functools.partial(body, rev), 0)

def specs(cb, first):
    g = cb // 8
    rows = lambda lanes: pl.BlockSpec((cb, lanes), lambda i: (i + first, 0))
    per = lambda a, b: pl.BlockSpec((g, a, b), lambda i: (i + first, 0, 0))
    flat = lambda lanes: pl.BlockSpec((g, lanes), lambda i: (i + first, 0))
    return rows, per, flat

def mix_call(kernel, name, out_shape, in_specs, out_specs, steps, done, args):
    n = len(args)
    if done is None:
        body, aliases, done = kernel, {}, ()
    else:
        body = lambda *refs: kernel(*refs[:n], *refs[n + len(done):])
        aliases = {n + i: i for i in range(len(done))}
        in_specs = in_specs + [pl.BlockSpec(memory_space=pl.ANY)] * len(done)
    return pl.pallas_call(
        body,
        out_shape=out_shape,
        grid=(steps,),
        in_specs=in_specs,
        out_specs=out_specs,
        input_output_aliases=aliases,
        compiler_params=pltpu.CompilerParams(vmem_limit_bytes=60 << 20),
        name=name,
    )(*args, *done)

MASKS = pl.BlockSpec((8, 256), lambda i: (0, 0))
SCALAR = pl.BlockSpec(memory_space=pltpu.SMEM)

def ssm_fwd(direction, x, d3, w3, drow, wrow, skip, masks, part=0, parts=1, done=None, cb=64, unroll=8):
    c, tok = x.shape
    steps = c // cb // parts
    rows, per, flat = specs(cb, part * steps)
    return mix_call(
        functools.partial(fwd_kernel, cb // 8, unroll),
        f"mix_forward_{part}",
        (jax.ShapeDtypeStruct((c, tok), f32), jax.ShapeDtypeStruct((c // 8, 64, 256), f32)),
        [SCALAR, rows(tok), per(24, 64), per(24, 64), flat(512), flat(512), rows(1), MASKS],
        (rows(tok), per(64, 256)),
        steps, done, (direction, x, d3, w3, drow, wrow, skip, masks),
    )

def ssm_bwd(direction, x, gm, enter, d3, w3, drow, skip, masks, part=0, parts=1, done=None, cb=128, unroll=8):
    c, tok = x.shape
    steps = c // cb // parts
    first = part * steps
    rows, per, flat = specs(cb, first)
    return mix_call(
        functools.partial(bwd_kernel, cb // 8, unroll),
        f"mix_backward_{part}",
        (jax.ShapeDtypeStruct((c, tok), bf16), jax.ShapeDtypeStruct((128, c), f32), jax.ShapeDtypeStruct((c, 1), f32), jax.ShapeDtypeStruct((c, 1), f32)),
        [SCALAR, rows(tok), rows(tok), per(64, 256), per(24, 64), per(24, 64), flat(512), rows(1), MASKS],
        (rows(tok), pl.BlockSpec((128, cb), lambda i: (0, i + first)), rows(1), rows(1)),
        steps, done, (direction, x, gm, enter, d3, w3, drow, skip, masks),
    )

def thirds(x):
    hi = x.astype(bf16)
    rest = x - hi.astype(f32)
    mid = rest.astype(bf16)
    lo = (rest - mid.astype(f32)).astype(bf16)
    c = x.shape[0]
    return jnp.concatenate([a.reshape(c // 8, 8, 64) for a in (hi, mid, lo)], 1)

def block_masks(labels, rev):
    idx = jnp.arange(16)[None, :]
    def reach(k, back):
        other = jnp.roll(labels, -k if back else k, axis=1)
        inside = (idx + k < 16) if back else (idx >= k)
        return (inside & (other == labels)).astype(f32).reshape(32)
    ahead = jnp.stack([reach(k, False) for k in (1, 2, 4, 8)])
    behind = jnp.stack([reach(k, True) for k in (1, 2, 4, 8)])
    both = jnp.where(rev, jnp.concatenate([behind, ahead]), jnp.concatenate([ahead, behind]))
    return jnp.tile(both, (1, 8))


ROUNDS = (
    {"y": "own", "z": "own", "x": "own", "o": "own", "m": "own"},
    {"z": (0, "m"), "m": (0, "z"), "y": (0, "x"), "x": (0, "z"), "o": (0, "y")},
    {"x": (1, "z"), "m": (1, "z"), "y": (1, "z"), "z": (1, "m"), "o": (1, "z")},
    {"z": (0, "y"), "y": (2, "z"), "m": (2, "x"), "x": (2, "z"), "o": (0, "z")},
    {"x": (3, "y"), "o": (3, "x"), "y": (2, "x"), "z": (1, "y")},
)
PERMS = {
    "x": [(w, w ^ 1) for w in range(16)],
    "y": [(w, w ^ 2) for w in range(16)],
    "z": [(w, w ^ 4) for w in range(16)],
    "m": [(w, w + 4) for w in range(4, 8)] + [(w, w - 4) for w in range(8, 12)],
}


def trace_rounds():
    end, mid = {"own": (0, 0, 0)}, {"own": (0, 0, 1)}
    for r, sends in enumerate(ROUNDS):
        new_end, new_mid = {}, {}
        for d, bit in (("x", 0), ("y", 1)):
            for held, new in ((end, new_end), (mid, new_mid)):
                item = list(held[sends[d]])
                item[bit] ^= 1
                new[(r, d)] = tuple(item)
        new_end[(r, "z")], new_mid[(r, "z")] = mid[sends["z"]], end[sends["o"]]
        if "m" in sends:
            dx, dy, layer = mid[sends["m"]]
            new_end[(r, "m")], new_mid[(r, "m")] = None, (dx, dy, 3 - layer)
        end.update(new_end)
        mid.update(new_mid)

    def firsts(held):
        seen, first = set(), {}
        for slot, item in held.items():
            first[slot] = item is not None and item not in seen
            seen.add(item)
        return first

    return end, mid, firsts(end), firsts(mid)


END, MID, FIRST_END, FIRST_MID = trace_rounds()
SLOTS = tuple(END)


def at_end():
    layer = lax.axis_index("wide") >> 2
    return (layer == 0) | (layer == 3)


def owner(slot):
    w = lax.axis_index("wide")
    x, y, layer = w & 1, (w >> 1) & 1, w >> 2

    def of(held):
        dx, dy, z = held[slot] or (0, 0, 0)
        return jnp.where(layer >= 2, 3 - z, z) * 4 + (y ^ dy) * 2 + (x ^ dx)

    return jnp.where(at_end(), of(END), of(MID))


def is_first(slot):
    return jnp.where(at_end(), int(FIRST_END[slot]), int(FIRST_MID[slot]))


def core_index():
    return lax.axis_index("narrow") & 1


def within_half(w, rows):
    return pl.multiple_of((w & 7) * rows, 16)


ANY = pl.BlockSpec(memory_space=pl.ANY)
HBM = pl.BlockSpec(memory_space=pltpu.HBM)
VM = pl.BlockSpec(memory_space=pltpu.VMEM)


def params(mib=60):
    return pltpu.CompilerParams(vmem_limit_bytes=mib << 20)


def shape(dims, dtype):
    return jax.ShapeDtypeStruct(dims, dtype)


def ones_where(condition):
    return jnp.where(condition, 1.0, 0.0).astype(bf16)


def pack_kernel(up, value, proj, out, rate, in_map, out_map, vectors, keep, send, rows):
    def lanes(n, first):
        return ones_where(iota((n, 256), 1) == iota((n, 256), 0) + first)

    rows[...] = jnp.zeros((16, 48), f32)
    for k in range(6):
        rows[k : k + 1, :] = vectors[:, 48 * k : 48 * k + 48]
    for k, n in enumerate((24, 24, 24, 16)):
        rows[6 + k : 7 + k, :n] = vectors[:, 288 + 24 * k : 288 + 24 * k + n]
    small = dot(rows[...].astype(bf16), lanes(16, 192), ((0,), (0,)))
    for k, ref in enumerate((rate, in_map, out_map)):
        small = small + dot(ref[...], lanes(64, 64 * k))
    for core in range(2):

        @pl.when(core_index() == core)
        def _(core=core):
            for ref, half in ((keep, core), (send, 1 - core)):
                a = up[...].astype(f32)
                for q in range(2):
                    ref[24 * q : 24 * q + 24, :] = a[:, 1536 * half + 768 * q : 1536 * half + 768 * q + 768]
                ref[48:72, :] = value[...].astype(f32)[:, 768 * half : 768 * half + 768]
                ref[72:168, :] = proj[...].astype(f32)[:, 768 * half : 768 * half + 768]
                b = out[...].astype(f32)[:, 384 * half : 384 * half + 384]
                ref[168:192, :384] = b[:24]
                ref[168:192, 384:] = b[24:]
                for j in range(3):
                    ref[192:208, 256 * j : 256 * j + 256] = small[16 * j : 16 * j + 16, :]


def pack(*shards):
    return pl.pallas_call(
        pack_kernel,
        out_shape=(shape((208, 768), f32),) * 2,
        in_specs=[VM] * len(shards),
        out_specs=(VM, VM),
        scratch_shapes=[pltpu.VMEM((16, 48), f32)],
        compiler_params=params(),
        name="pack_shards",
    )(*shards)


def merge_kernel(keep, recv, blob):
    for core in range(2):

        @pl.when(core_index() == core)
        def _(core=core):
            lo, hi = (keep, recv) if core == 0 else (recv, keep)

            def both(a, n):
                return jnp.concatenate([lo[a : a + n, :], hi[a : a + n, :]], 0)

            for q in range(2):
                blob[48 * q : 48 * q + 48, :] = both(24 * q, 24).astype(bf16)
            blob[96:144, :] = both(48, 24).astype(bf16)
            s = [ref[192:208, 256 * j : 256 * j + 256] for ref in (lo, hi) for j in range(3)]
            for j in range(3):
                blob[144:176, 256 * j : 256 * j + 256] = jnp.concatenate(s[2 * j : 2 * j + 2], 0).astype(bf16)
            blob[176:368, :] = both(72, 96).astype(bf16)
            for k, ref in enumerate((lo, hi)):
                rows = jnp.concatenate([ref[168:192, :384], ref[168:192, 384:]], 0)
                blob[368:416, 384 * k : 384 * k + 384] = rows.astype(bf16)


def merge(keep, recv):
    return pl.pallas_call(
        merge_kernel,
        out_shape=shape((416, 768), bf16),
        in_specs=[VM, VM],
        out_specs=VM,
        compiler_params=params(),
        name="merge_pair",
    )(keep, recv)


def together(*trees):
    return lax.optimization_barrier(trees)


def gather_rounds(own, work, state=None):
    held = {"own": own}
    end = at_end()
    for r, sends in enumerate(ROUNDS):
        blocks = {}
        for d in "xyzm":
            if d in sends:
                block = held[sends[d]]
                if d == "z" and sends["z"] != sends["o"]:
                    block = jnp.where(end, held[sends["o"]], block)
                blocks[d] = block
        blocks, state = together(blocks, state)
        came = {d: lax.ppermute(block, "wide", PERMS[d]) for d, block in blocks.items()}
        state = work[r](state)
        if r == len(ROUNDS) - 1:
            early = dict(held)
            early[sends["x"]] = blocks["x"]
            placed = place_all(tuple(early), tuple(early.values()))
            came, placed, state = together(came, placed, state)
            late = {(r, d): block for d, block in came.items()}
            return place_all(tuple(late), tuple(late.values()), placed), state
        came, state = together(came, state)
        held.update({(r, d): block for d, block in came.items()})


def place_kernel(slots, pieces, outs, held, *refs):
    n = len(slots)
    blocks, refs = refs[:n], refs[n + held :]
    dests, (buf, in_sem, out_sem) = refs[:outs], refs[outs:]

    def each_slot(act):
        for i, slot in enumerate(slots):
            if FIRST_END[slot] and FIRST_MID[slot]:
                act(i, owner(slot))
            else:
                pl.when(is_first(slot) == 1)(functools.partial(act, i, owner(slot)))

    def load(i):
        return pltpu.make_async_copy(blocks[i], buf.at[i], in_sem.at[i])

    def stores(i, w):
        mine = (w >> 3) == core_index()
        for src, which, dst in pieces:

            def go(at, src=src, dst=dst):
                pltpu.make_async_copy(buf.at[(i,) + src], dests[at].at[dst(w)], out_sem.at[i]).start()

            if isinstance(which, int):
                go(which)
            else:
                pl.when(mine)(functools.partial(go, which[0]))
                pl.when(jnp.logical_not(mine))(functools.partial(go, which[1]))

    def load_start(i, w):
        load(i).start()

    def pass_on(i, w):
        load(i).wait()
        stores(i, w)

    def finish(i, w):
        pltpu.make_async_copy(blocks[i], buf.at[i], out_sem.at[i]).wait()

    for act in (load_start, pass_on, finish):
        each_slot(act)


def place(slots, blocks, pieces, out_shapes, done, name):
    n, held = len(slots), len(done)
    return pl.pallas_call(
        functools.partial(place_kernel, slots, pieces, len(out_shapes), held),
        out_shape=out_shapes,
        in_specs=[ANY] * (n + held),
        out_specs=tuple(ANY for _ in out_shapes),
        input_output_aliases={n + k: k for k in range(held)},
        scratch_shapes=[
            pltpu.VMEM((n,) + blocks[0].shape, bf16),
            pltpu.SemaphoreType.DMA((n,)),
            pltpu.SemaphoreType.DMA((n,)),
        ],
        compiler_params=params(),
        name=name,
    )(*blocks, *done)


def place_all(slots, blocks, done=()):
    full = slice(None)
    pieces = [
        ((slice(0, 48), full), 0, lambda w: (pl.ds(pl.multiple_of(w * 48, 16), 48), slice(0, 768))),
        ((slice(48, 96), full), 0, lambda w: (pl.ds(pl.multiple_of(w * 48, 16), 48), slice(768, 1536))),
        ((slice(96, 144), full), 1, lambda w: (pl.ds(pl.multiple_of(w * 48, 16), 48), full)),
        ((slice(176, 368), full), (3, 4), lambda w: (pl.ds(within_half(w, 192), 192), full)),
    ]
    for j in range(3):
        pieces.append(
            (
                (slice(144, 176), slice(256 * j, 256 * j + 256)),
                2,
                lambda w, j=j: (pl.ds(pl.multiple_of(w * 96 + 32 * j, 16), 32), full),
            )
        )
    for k in range(2):
        pieces.append(
            (
                (slice(368, 416), slice(384 * k, 384 * k + 384)),
                (5, 6),
                lambda w, k=k: (pl.ds(within_half(w, 96) + 48 * k, 48), full),
            )
        )
    dims = ((768, 1536), (768, 768), (1536, 256), (1536, 768), (1536, 768), (768, 384), (768, 384))
    name = "place_last" if done else "place_first"
    return place(slots, blocks, pieces, tuple(shape(d, bf16) for d in dims), done, name)


def divided_by_48(x):
    return (x * 1366) >> 16


def row_of_wide(shape_of, width_dim):
    d = iota(shape_of, width_dim)
    w = divided_by_48(d)
    rest = d - 48 * w
    c = jnp.where(rest >= 24, 1, 0)
    return 96 * w + 48 * c + rest - 24 * c


def row_of_up(shape_of, up_dim):
    f = iota(shape_of, up_dim)
    q = divided_by_48(f)
    return 96 * (q >> 2) + 48 * ((q >> 1) & 1) + f - 48 * q, q & 1


def mix_parameters(mine):
    rate = -jnp.exp(mine[:, :64])
    step = jnp.exp(mine[:, 192:193])
    decay_log = step * rate
    decay = jnp.exp(decay_log)
    gap = (decay - 1.0) / rate
    return rate, step, decay_log, decay, gap


def coefficients_kernel(table, labels, d3, w3, drow, wrow, skip, value_b, proj_b, up_b, wide, masks, buf):
    half = pl.ds(pl.multiple_of(core_index() * 768, 256), 768)
    mine = table[half, :].astype(f32)
    rate, step, decay_log, decay, gap = mix_parameters(mine)
    weight = mine[:, 128:192] * gap * mine[:, 64:128]
    for v, three, row in ((decay_log, d3, drow), (weight, w3, wrow)):
        rest = v
        for k in range(3):
            part = rest.astype(bf16)
            three[:, 8 * k : 8 * k + 8, :] = part.reshape(96, 8, 64)
            rest = rest - part.astype(f32)
        buf[...] = v
        for c in range(8):
            row[:, 64 * c : 64 * c + 64] = buf[pl.ds(c, 96, stride=8), :]
    skip[...] = mine[:, 193:194]
    value_b[...] = mine[:, 194:195]
    low = table[half, 128:]
    proj_b[...] = mine[:, 128:].T[67:68, :]
    r, k = row_of_up((768, 1536), 1)
    at = r == iota((768, 1536), 0)
    pick = lambda which: dot(low, ones_where(at & (k == which)), ((0,), (0,)))
    up_b[...] = pick(0)[68:69, :] + pick(1)[69:70, :]
    spread_wide = ones_where(row_of_wide((1536, 768), 1) == iota((1536, 768), 0))
    wide[...] = dot(table[:, 128:], spread_wide, ((0,), (0,)))[70:73, :]
    lane = iota((8, 256), 1)
    each_lane = ones_where((iota((32, 256), 1) & 31) == iota((32, 256), 0))
    label = dot(jnp.broadcast_to(labels[...], (8, 32)).astype(bf16), each_lane)
    rows = []
    for k in (1, 2, 4, 8):
        before = jnp.where(((lane & 15) >= k) & (roll_halves(label, k) == label), 1.0, 0.0)
        behind = jnp.where(((lane & 15) + k < 16) & (roll_halves(label, 128 - k) == label), 1.0, 0.0)
        rows.append((before, behind))
    back = core_index() == 1
    for i, (before, behind) in enumerate(rows):
        masks[i : i + 1, :] = jnp.where(back, behind, before)[:1]
        masks[4 + i : 5 + i, :] = jnp.where(back, before, behind)[:1]


def coefficients(table, labels):
    dims = [((96, 24, 64), bf16)] * 2 + [((96, 512), f32)] * 2 + [((768, 1), f32)] * 2 + [((1, 768), f32), ((1, 1536), f32), ((3, 768), f32), ((8, 256), f32)]
    return pl.pallas_call(
        coefficients_kernel,
        out_shape=tuple(shape(*d) for d in dims),
        in_specs=[VM, VM],
        out_specs=(VM,) * len(dims),
        scratch_shapes=[pltpu.VMEM((768, 64), f32)],
        compiler_params=params(),
        name="coefficients",
    )(table, labels)


def small_sums_kernel(table, grads, skip, value_b, proj_b, up_b, gain, shift, out_b, out, buf, turn_buf):
    half = pl.ds(pl.multiple_of(core_index() * 768, 256), 768)
    theirs = pl.ds(pl.multiple_of((1 - core_index()) * 768, 256), 768)
    mine = table[half, :].astype(f32)
    rate, step, decay_log, decay, gap = mix_parameters(mine)
    in_p, out_p = mine[:, 64:128], mine[:, 128:192]
    both = grads[...].T
    weight, slope = both[:, :64], both[:, 64:]
    product = out_p * in_p
    through = slope * decay_log
    buf[theirs, :] = jnp.zeros((768, 256), f32)
    buf[half, 128:] = jnp.zeros((768, 128), f32)
    turn_buf[...] = jnp.zeros((128, 128), f32)
    buf[half, 0:64] = through + weight * (product * (decay * step - gap))
    buf[half, 64:128] = weight * out_p * gap
    buf[half, 128:192] = weight * in_p * gap
    buf[half, 192:193] = jnp.sum(through + weight * (product * decay * step), axis=1, keepdims=True)
    for k, ref in enumerate((skip, value_b)):
        buf[half, 193 + k : 194 + k] = ref[...]
    buf[half, 195:196] = jnp.broadcast_to(proj_b[...], (8, 768)).T[:, :1]
    for q in range(32):
        turn_buf[q : q + 1, 0:48] = up_b[:, 48 * q : 48 * q + 48]
        for k, ref in enumerate((gain, shift, out_b)):
            turn_buf[32 + 3 * q + k : 33 + 3 * q + k, 0:24] = ref[:, 24 * q : 24 * q + 24]
    columns = turn_buf[...].T
    for q in range(16):
        buf[pl.ds(pl.multiple_of(core_index() * 768 + 48 * q, 16), 48), 196:198] = columns[:48, 2 * q : 2 * q + 2]
    for q in range(32):
        buf[48 * q : 48 * q + 24, 198:201] = columns[:24, 32 + 3 * q : 35 + 3 * q]
    for w in range(16):
        for j in range(3):
            out[w, :, 256 * j : 256 * j + 256] = buf[96 * w + 32 * j : 96 * w + 32 * j + 32, :]


def small_sums(*args):
    return pl.pallas_call(
        small_sums_kernel,
        out_shape=shape((16, 32, 768), f32),
        in_specs=[VM] * len(args),
        out_specs=VM,
        scratch_shapes=[pltpu.VMEM((1536, 256), f32), pltpu.VMEM((128, 128), f32)],
        compiler_params=params(),
        name="small_sums",
    )(*args)


def children_of():
    kids = {s: [] for s in SLOTS}
    for r, sends in enumerate(ROUNDS):
        for d in "xyzm":
            if d not in sends:
                continue
            if d != "z" or sends["z"] == sends["o"]:
                kids[sends[d]].append(((r, d), None))
            else:
                kids[sends["z"]].append(((r, "z"), "mid"))
                kids[sends["o"]].append(((r, "z"), "end"))
    return kids


KIDS = children_of()


def sum_kernel(slots, pieces, n_own, arrived, rows, final, *refs):
    owns, refs = refs[:n_own], refs[n_own:]
    ins, refs = refs[: len(arrived)], refs[len(arrived) :]
    n_out = 2 if final else len(slots)
    outs, (own_buf, small_buf, in_buf, out_buf, own_sem, small_sem, in_sem, out_sem) = refs[:n_out], refs[n_out:]
    in_copies = []

    def start_own(p):
        w = owner(slots[p])
        mine = (w >> 3) == core_index()
        for choices, dst in pieces:
            for choice, (which, src) in enumerate(choices):

                def go(which=which, src=src, dst=dst):
                    buf, sem = (own_buf, own_sem) if owns[which].dtype == bf16 else (small_buf, small_sem)
                    pltpu.make_async_copy(owns[which].at[src(w)], buf.at[(p,) + dst], sem.at[p]).start()

                if len(choices) == 1:
                    go()
                else:
                    pl.when(mine == (choice == 0))(go)

    def wait_own(p):
        for buf, sem in ((own_buf, own_sem), (small_buf, small_sem)):
            pltpu.make_async_copy(buf.at[p], buf.at[p], sem.at[p]).wait()

    for p in range(len(slots)):
        start_own(p)
    for k in range(len(arrived)):
        in_copies.append(pltpu.make_async_copy(ins[k], in_buf.at[k], in_sem.at[k]))
        in_copies[-1].start()
    end = at_end()
    waited = set()
    sent = []
    for p, slot in enumerate(slots):
        wait_own(p)
        parts = []
        for kid, layers in KIDS[slot]:
            k = arrived.index(kid)
            if k not in waited:
                in_copies[k].wait()
                waited.add(k)
            parts.append((k, None if layers is None else jnp.where(end == (layers == "end"), 1.0, 0.0)))
        whole = FIRST_END[slot] and FIRST_MID[slot]
        keep = None if whole else is_first(slot).astype(f32)

        def add(i, _, p=p, parts=parts, keep=keep, own=own_buf, first=0):
            at = pl.ds(pl.multiple_of(i * 32, 32), 32)
            to = pl.ds(pl.multiple_of(first + i * 32, 32), 32)
            total = own[p, at, :].astype(f32)
            if keep is not None:
                total = total * keep
            for k, mask in parts:
                v = in_buf[k, to, :].astype(f32)
                total = total + (v if mask is None else v * mask)
            out_buf[p, to, :] = total.astype(out_buf.dtype)
            return 0

        low_rows, small_rows = own_buf.shape[1], small_buf.shape[1]
        lax.fori_loop(0, low_rows // 32, add, 0, unroll=4)
        lax.fori_loop(0, small_rows // 32, functools.partial(add, own=small_buf, first=low_rows), 0)
        if not final:
            sent.append(pltpu.make_async_copy(out_buf.at[p], outs[p], out_sem.at[p]))
            sent[-1].start()
    if final:
        for i, (ref, core) in enumerate(((outs[0], core_index()), (outs[1], 1 - core_index()))):
            for k, (src, dst) in enumerate(final):
                sent.append(pltpu.make_async_copy(out_buf.at[(0,) + src(core)], ref.at[dst], out_sem.at[i * len(final) + k]))
                sent[-1].start()
    for c in sent:
        c.wait()


def sum_slots(slots, owns, pieces, came, rows, final=None, final_rows=None, name="sum"):
    arrived = []
    for slot in slots:
        for kid, _ in KIDS[slot]:
            if kid not in arrived:
                arrived.append(kid)
    if final:
        out_shapes = (shape((final_rows, 768), f32),) * 2
    else:
        out_shapes = tuple(shape((rows, 768), bf16) for _ in slots)
    return pl.pallas_call(
        functools.partial(sum_kernel, slots, pieces, len(owns), arrived, rows, final),
        out_shape=out_shapes,
        in_specs=[ANY] * (len(owns) + len(arrived)),
        out_specs=tuple(HBM for _ in out_shapes),
        scratch_shapes=[
            pltpu.VMEM((len(slots), rows - 32, 768), bf16),
            pltpu.VMEM((len(slots), 32, 768), f32),
            pltpu.VMEM((max(1, len(arrived)), rows, 768), bf16),
            pltpu.VMEM((len(slots), rows, 768), f32 if final else bf16),
            pltpu.SemaphoreType.DMA((len(slots),)),
            pltpu.SemaphoreType.DMA((len(slots),)),
            pltpu.SemaphoreType.DMA((max(1, len(arrived)),)),
            pltpu.SemaphoreType.DMA((2 * len(final) if final else len(slots),)),
        ],
        compiler_params=params(),
        name=name,
    )(*owns, *[came[k] for k in arrived])


def scatter_rounds(owns, pieces, rows, final, final_rows, name, work, state=None):
    came = {}
    for r in reversed(range(len(ROUNDS))):
        slots = [(r, d) for d in "xyzm" if d in ROUNDS[r]]
        blocks = sum_slots(slots, owns, pieces, came, rows, name=f"{name}_{r}")
        blocks, state = together(blocks, state)
        new = {slot: lax.ppermute(block, "wide", PERMS[slot[1]]) for slot, block in zip(slots, blocks)}
        state = work[len(ROUNDS) - 1 - r](state)
        new, state = together(new, state)
        came.update(new)
    return sum_slots(["own"], owns, pieces, came, rows, final, final_rows, name=f"{name}_own"), state


def scatter_all(proj_mine, proj_theirs, out, out_theirs, up, value, small, work, state):
    full = slice(None)

    def lanes():
        return pl.ds(pl.multiple_of(core_index() * 384, 128), 384)

    pieces = [([(i, lambda w: (pl.ds(within_half(w, 192), 192), full)) for i in (0, 1)], (slice(0, 192), full))]
    for k in range(2):
        pieces.append(
            (
                [
                    (2, lambda w, k=k: (pl.ds(within_half(w, 96) + 48 * k, 48), lanes())),
                    (3, lambda w, k=k: (pl.ds(within_half(w, 96) + 48 * k, 48), full)),
                ],
                (slice(192, 240), slice(384 * k, 384 * k + 384)),
            )
        )
        pieces.append(
            (
                [(4, lambda w, k=k: (pl.ds(pl.multiple_of(w * 48, 16), 48), slice(768 * k, 768 * k + 768)))],
                (slice(240 + 48 * k, 288 + 48 * k), full),
            )
        )
    pieces.append(([(5, lambda w: (pl.ds(pl.multiple_of(w * 48, 16), 48), full))], (slice(336, 384), full)))
    pieces.append(([(6, lambda w: (w,))], (slice(0, 32), full)))
    final = [
        (lambda c: (pl.ds(pl.multiple_of(c * 96, 8), 96), full), (slice(0, 96), full)),
        (lambda c: (slice(192, 240), pl.ds(pl.multiple_of(c * 384, 128), 384)), (slice(96, 144), slice(0, 384))),
        (lambda c: (slice(384, 416), full), (slice(216, 248), full)),
    ] + [
        (
            lambda c, q=q: (pl.ds(pl.multiple_of(240 + q * 48 + c * 24, 8), 24), full),
            (slice(144 + 24 * q, 168 + 24 * q), full),
        )
        for q in range(3)
    ]
    owns = (proj_mine, proj_theirs, out, out_theirs, up, value, small)
    return scatter_rounds(owns, pieces, 416, final, 248, "sum", work, state)


def unpack_kernel(mine, recv, proj, out, up, value, rate, in_map, out_map, vectors, small):
    for core in range(2):

        @pl.when(core_index() == core)
        def _(core=core):
            for ref, half in ((mine, core), (recv, 1 - core)):
                proj[:, 768 * half : 768 * half + 768] = ref[:96, :]
                out[:, 384 * half : 384 * half + 384] = ref[96:144, :384]
                for q in range(2):
                    up[:, 1536 * half + 768 * q : 1536 * half + 768 * q + 768] = ref[144 + 24 * q : 168 + 24 * q, :]
                value[:, 768 * half : 768 * half + 768] = ref[192:216, :]
            s = mine[216:248, :] + recv[216:248, :]
            if core == 0:
                small[:32, :] = s[:, :256]
                small[32:, :] = s[:16, 256:512]
            else:
                small[:16, :] = s[16:, 256:512]
                small[16:, :] = s[:, 512:]

    rate[...] = small[:, :64]
    in_map[...] = small[:, 64:128]
    out_map[...] = small[:, 128:192]
    vectors[...] = small[:, 128:].T[64:80, :]


def unpack(mine, recv):
    dims = ((96, 1536), (48, 768), (24, 3072), (24, 1536), (48, 64), (48, 64), (48, 64), (16, 48))
    return pl.pallas_call(
        unpack_kernel,
        out_shape=tuple(shape(d, f32) for d in dims),
        in_specs=[VM, VM],
        out_specs=(VM,) * len(dims),
        scratch_shapes=[pltpu.VMEM((48, 256), f32)],
        compiler_params=params(),
        name="unpack_sums",
    )(mine, recv)


TILE = 256


def tokens_by(width):
    return pl.BlockSpec((TILE, width), lambda i: (i, 0))


def by_tokens(rows):
    return pl.BlockSpec((rows, TILE), lambda i: (0, i))


def whole_block(*dims):
    return pl.BlockSpec(dims, lambda i: (0,) * len(dims))


def enter_kernel(unit, wide, up_w, up_b, value_w, value_b, normed, up_pre, up_low, value_pre):
    low = (unit[...] * wide[0:1, :] + wide[1:2, :]).astype(bf16)
    normed[...] = low
    value_pre[...] = dot(low, value_w[...]).T + value_b[...]
    for k in range(0, up_w.shape[1], 512):
        at = slice(k, k + 512)
        pre = dot(low, up_w[:, at]) + up_b[:, at]
        up_pre[:, at] = pre
        up_low[:, at] = gelu(pre).astype(bf16)


def enter(unit, wide, up_w, up_b, value_w, value_b):
    n, d = unit.shape
    f, c = up_w.shape[1], value_w.shape[1]
    return pl.pallas_call(
        enter_kernel,
        out_shape=(shape((n, d), bf16), shape((n, f), f32), shape((n, f), bf16), shape((c, n), f32)),
        grid=(n // TILE,),
        in_specs=[tokens_by(d)] + [whole_block(*v.shape) for v in (wide, up_w, up_b, value_w, value_b)],
        out_specs=(tokens_by(d), tokens_by(f), tokens_by(f), by_tokens(c)),
        compiler_params=params(),
        name="enter",
    )(unit, wide, up_w, up_b, value_w, value_b)


def gate_kernel(up, up_other, g, mixed, proj_mine, proj_theirs, proj_b, out_a, out_b, gm, gated, gp, grad_b, grad_mine, grad_theirs, grad_out, acc, acc_out, out_w):
    step, steps = pl.program_id(0), pl.num_programs(0)

    @pl.when(step == 0)
    def _():
        acc[...] = jnp.zeros_like(acc)
        acc_out[...] = jnp.zeros_like(acc_out)
        grad_b[...] = jnp.zeros_like(grad_b)
        for core in range(2):

            @pl.when(core_index() == core)
            def _(core=core):
                out_w[:, 384 * core : 384 * core + 384] = out_a[...]
                out_w[:, 384 - 384 * core : 768 - 384 * core] = out_b[...]

    proj = dot(up[...], proj_mine[...]) + dot(up_other[...], proj_theirs[...]) + proj_b[...]
    gg = dot(g[...], out_w[...], ((1,), (1,)))
    gm[...] = (gg * proj).T
    mix = mixed[...].T
    low = (mix * proj).astype(bf16)
    gated[...] = low
    gp_low = (gg * mix).astype(bf16)
    gp[...] = gp_low
    grad_b[...] += jnp.sum(gp_low.astype(f32), axis=0, keepdims=True)
    for k, ref in enumerate((up, up_other)):
        acc[k] += dot(ref[...], gp_low, ((0,), (0,)))
    acc_out[...] += dot(low, g[...], ((0,), (0,)))

    @pl.when(step == steps - 1)
    def _():
        grad_mine[...] = acc[0].astype(bf16)
        grad_theirs[...] = acc[1].astype(bf16)
        grad_out[...] = acc_out[...].astype(bf16)


def gate(up, up_other, g, mixed, proj_mine, proj_theirs, proj_b, out_a, out_b):
    n, f = up.shape
    c, d = out_a.shape[0], g.shape[1]
    return pl.pallas_call(
        gate_kernel,
        out_shape=(
            shape((c, n), f32),
            shape((n, c), bf16),
            shape((n, c), bf16),
            shape((1, c), f32),
            shape((f, c), bf16),
            shape((f, c), bf16),
            shape((c, d), bf16),
        ),
        grid=(n // TILE,),
        in_specs=[tokens_by(f), tokens_by(f), tokens_by(d), by_tokens(c)]
        + [whole_block(*v.shape) for v in (proj_mine, proj_theirs, proj_b, out_a, out_b)],
        out_specs=(by_tokens(c), tokens_by(c), tokens_by(c), whole_block(1, c))
        + (whole_block(f, c), whole_block(f, c), whole_block(c, d)),
        scratch_shapes=[pltpu.VMEM((2, f, c), f32), pltpu.VMEM((c, d), f32), pltpu.VMEM((c, d), bf16)],
        compiler_params=params(),
        name="gate",
    )(up, up_other, g, mixed, proj_mine, proj_theirs, proj_b, out_a, out_b)


def contract(left, right, left_dim, right_dim):
    return lax.dot_general(left, right, (((left_dim,), (right_dim,)), ((), ())), preferred_element_type=f32)


def by_core(core, zero, one):
    return jnp.where(core == 0, zero, one)


def in_order(core, mine, other, axis):
    return by_core(core, jnp.concatenate([mine, other], axis), jnp.concatenate([other, mine], axis))


def half_of(x, which, axis):
    size = x.shape[axis] // 2
    return lax.dynamic_slice_in_dim(x, which * size, size, axis)


def per_device(
    sizes,
    tokens,
    segment,
    cotangent,
    w_up,
    w_value,
    w_proj,
    w_out,
    norm_gain,
    norm_bias,
    bias_up,
    bias_value,
    bias_proj,
    bias_out,
    log_rate,
    log_step,
    input_map,
    output_map,
    skip_gain,
):
    both = ("wide", "narrow")
    core = core_index()
    pairs = [(i, i ^ 1) for i in range(sizes["narrow"])]
    staged = sizes["wide"] == 16 and sizes["narrow"] == 2

    def swap(x):
        return lax.ppermute(x, "narrow", pairs)

    tok, width = tokens.shape
    blocks = tok // T

    def by_place(x):
        return x.reshape(blocks, T, width).transpose(1, 0, 2)

    labels = segment.reshape(blocks, T)[:, 0].astype(f32)
    own_x, own_g = by_place(tokens), by_place(cotangent)

    def whole_chip(mine, other):
        return by_core(core, jnp.stack([mine, other], 1), jnp.stack([other, mine], 1)).reshape(2 * tok, width)

    def normalise(x):
        x = x.astype(f32)
        average = jnp.mean(x, axis=-1, keepdims=True)
        centred = x - average
        scale = lax.rsqrt(jnp.mean(centred * centred, axis=-1, keepdims=True) + 1e-05)
        return centred * scale, scale

    if staged:
        vectors = (log_step, skip_gain, bias_value, bias_proj, bias_up, norm_gain, norm_bias, bias_out, labels)
        vectors = jnp.concatenate([v.astype(f32) for v in vectors])[None]
        keep, send = pack(w_up, w_value, w_proj, w_out, log_rate, input_map, output_map, vectors)
        recv = swap(send)
        other_labels = recv[192:208, 201]
        blob = merge(keep, recv)
        other_x, other_g = swap(own_x), swap(own_g)
        idle = lambda state: state

        def chip_tokens(state):
            (mine_x, their_x), (mine_g, their_g) = state
            return whole_chip(mine_x, their_x), whole_chip(mine_g, their_g)

        def chip_unit(state):
            return normalise(state[0])[0], state[1]

        state = (own_x, other_x), (own_g, other_g)
        placed, (unit_chip, g_chip) = gather_rounds(blob, [idle, chip_tokens, chip_unit, idle, idle], state)
        up_w, value_w, table, proj_mine, proj_theirs, out_mine, out_theirs = placed
        proj_cross = swap(proj_theirs)
        out_cross = swap(out_theirs)
        out_w = in_order(core, out_mine, out_cross, 1)
        label_row = in_order(core, labels, other_labels, 0)[None]
        coefs = coefficients(table, label_row)
        decay3, weight3, decay_row, weight_row, skip_p, value_b, proj_b, up_b, wide, masks = coefs
    else:
        other_x, other_g = swap(own_x), swap(own_g)
        unit_chip, g_chip = normalise(whole_chip(own_x, other_x))[0], whole_chip(own_g, other_g)
        other_labels = swap(labels)
        whole = lambda p: lax.all_gather(p, both, axis=0, tiled=True)
        up_w = half_of(whole(w_up), core, 1)
        value_w = half_of(whole(w_value), core, 1)
        full = whole(w_proj)
        proj_mine = half_of(half_of(full, core, 1), core, 0)
        proj_theirs = half_of(half_of(full, core, 1), 1 - core, 0)
        proj_cross = half_of(half_of(full, 1 - core, 1), core, 0)
        out_w = half_of(whole(w_out), core, 0)
        out_mine, out_cross = half_of(out_w, core, 1), half_of(out_w, 1 - core, 1)
        rate_p, in_p, out_p = (half_of(whole(p).astype(f32), core, 0) for p in (log_rate, input_map, output_map))
        step_p, skip_p, value_b, proj_b = (
            half_of(whole(p).astype(f32), core, 0)[:, None] for p in (log_step, skip_gain, bias_value, bias_proj)
        )
        proj_b = proj_b.T
        up_b = half_of(whole(bias_up).astype(f32), core, 0)[None]
        wide = jnp.stack([whole(p).astype(f32) for p in (norm_gain, norm_bias, bias_out)])

    direction = core.astype(jnp.int32).reshape(1)
    if not staged:
        rate = -jnp.exp(rate_p)
        step = jnp.exp(step_p)
        decay_log = step * rate
        decay = jnp.exp(decay_log)
        gap = (decay - 1.0) / rate
        weight = out_p * gap * in_p
        masks = block_masks(in_order(core, labels[None], other_labels[None], 0), core == 1)
        decay_row, weight_row = (v.reshape(-1, 512) for v in (decay_log, weight))
        decay3, weight3 = thirds(decay_log), thirds(weight)
    normed_low, up_pre, up_low, value_pre = enter(unit_chip, wide, up_w, up_b, value_w, value_b)
    up_other = swap(up_low)
    mixed, entering = ssm_fwd(direction, value_pre, decay3, weight3, decay_row, weight_row, skip_p, masks)
    grad_mixed, gated_low, grad_proj_low, grad_proj_b, grad_proj_mine, grad_proj_theirs, grad_out_w = gate(
        up_low, up_other, g_chip, mixed, proj_mine, proj_theirs, proj_b, out_mine, out_cross
    )

    grad_proj_other = swap(grad_proj_low)
    grad_value_low, grad_mix, grad_skip, grad_value_b = ssm_bwd(
        direction, value_pre, grad_mixed, entering, decay3, weight3, decay_row, skip_p, masks
    )
    grad_up_act = contract(grad_proj_low, proj_mine, 1, 1) + contract(grad_proj_other, proj_cross, 1, 1)
    grad_up_low = (grad_up_act * gelu_grad(up_pre)).astype(bf16)
    grad_up_b = jnp.sum(grad_up_low.astype(f32), axis=0, keepdims=True)
    grad_up_w = contract(normed_low, grad_up_low, 0, 0).astype(bf16)
    grad_value_w = contract(normed_low, grad_value_low, 0, 1).astype(bf16)

    def own_and_theirs(x):
        x = x.reshape(T, 2, blocks, width)
        return lax.dynamic_index_in_dim(x, core, 1, False), lax.dynamic_index_in_dim(x, 1 - core, 1, False)

    def by_token(x):
        return x.transpose(1, 0, 2).reshape(tok, width)

    grad_part = contract(grad_up_low, up_w, 1, 1) + contract(grad_value_low, value_w, 0, 1)
    grad_gain = jnp.sum(grad_part * unit_chip, axis=0, keepdims=True)
    grad_shift = jnp.sum(grad_part, axis=0, keepdims=True)
    own_gf = own_g.astype(f32)
    grad_out_b = jnp.sum(own_gf, axis=(0, 1))[None]

    def split_parts(state):
        gated, part = state
        mine, theirs = zip(own_and_theirs(contract(gated, out_w, 1, 0)), own_and_theirs(part))
        return mine, jnp.stack([t.astype(bf16) for t in theirs])

    def exchange_parts(state):
        return state[0], swap(state[1])

    def finish_result(state):
        mine, came = state
        return by_token((own_x.astype(f32) + mine[0] + came[0] + wide[2]).astype(bf16)), mine[1] + came[1]

    def finish_tokens(state):
        result, grad_normed = state
        unit, scale = normalise(own_x)
        h = grad_normed * wide[0]
        inner = h - jnp.mean(h, axis=-1, keepdims=True) - unit * jnp.mean(h * unit, axis=-1, keepdims=True)
        return result, by_token(own_gf + inner * scale)

    if staged:
        vectors = (grad_skip, grad_value_b, grad_proj_b, grad_up_b, grad_gain, grad_shift, grad_out_b)
        small = small_sums(table, grad_mix, *vectors)
        theirs = swap(half_of(grad_out_w, 1 - core, 1))
        work = [split_parts, exchange_parts, finish_result, finish_tokens, idle]
        grads = (grad_proj_mine, grad_proj_theirs, grad_out_w, theirs, grad_up_w, grad_value_w, small)
        (mine, send), (result, grad_tokens) = scatter_all(*grads, work, (gated_low, grad_part))
        sum_proj_w, sum_out_w, sum_up_w, sum_value_w, sum_rate, sum_in, sum_out, sums = unpack(mine, swap(send))
        sum_step, sum_skip, sum_value_b, sum_proj_b = (sums[k] for k in range(4))
        sum_up_b = sums[4:6].reshape(96)
        sum_gain, sum_shift, sum_out_b = (sums[6 + k, :24] for k in range(3))
    else:

        grad_mix = grad_mix.T
        grad_weight, grad_decay = grad_mix[:, :64], grad_mix[:, 64:]
        product = out_p * in_p
        grad_ssm = (
            grad_decay * decay_log + grad_weight * (product * (decay * step - gap)),
            grad_weight * out_p * gap,
            grad_weight * in_p * gap,
            jnp.sum(grad_decay * decay_log + grad_weight * (product * decay * step), axis=1, keepdims=True),
        )

        def share(x):
            return lax.psum_scatter(x.astype(f32), both, scatter_dimension=0, tiled=True)

        def halves(x, axis):
            zero = jnp.zeros_like(x)
            return share(in_order(core, x, zero, axis))

        result, grad_tokens = finish_tokens(finish_result(exchange_parts(split_parts((gated_low, grad_part)))))
        sum_up_w, sum_value_w = halves(grad_up_w, 1), halves(grad_value_w, 1)
        sum_proj_w = halves(in_order(core, grad_proj_mine, grad_proj_theirs, 0), 1)
        sum_out_w = halves(grad_out_w, 0)
        sum_rate, sum_in, sum_out, sum_step = (halves(v, 0) for v in grad_ssm)
        sum_step = sum_step[:, 0]
        sum_skip, sum_value_b, sum_proj_b = (halves(v, 0) for v in (grad_skip[:, 0], grad_value_b[:, 0], grad_proj_b[0]))
        sum_up_b = halves(grad_up_b[0], 0)
        sum_gain, sum_shift, sum_out_b = share(grad_gain[0]), share(grad_shift[0]), share(grad_out_b[0])

    return (
        result,
        grad_tokens,
        sum_up_w,
        sum_value_w,
        sum_proj_w,
        sum_out_w,
        sum_gain,
        sum_shift,
        sum_up_b,
        sum_value_b,
        sum_proj_b,
        sum_out_b,
        sum_rate,
        sum_step,
        sum_in,
        sum_out,
        sum_skip,
    )


def solution(mesh):
    rows, vector = P(("wide", "narrow"), None), P(("wide", "narrow"))
    sizes = dict(mesh.shape)
    return jax.shard_map(
        functools.partial(per_device, sizes),
        mesh=mesh,
        in_specs=(rows, vector, rows, rows, rows, rows, rows) + (vector,) * 6 + (rows, vector, rows, rows, vector),
        out_specs=(rows,) * 6 + (vector,) * 6 + (rows, vector, rows, rows, vector),
        check_vma=False,
    )
```

```python
import functools

import jax
import jax.numpy as jnp
from jax import lax
from jax.experimental import pallas as pl
from jax.experimental.pallas import tpu as pltpu
from jax.sharding import PartitionSpec as P

T = 32
NB = 32
f32, bf16 = jnp.float32, jnp.bfloat16

def iota(shape, dim): return lax.broadcasted_iota(jnp.int32, shape, dim)

def take(x, index, axis):
    return jnp.take_along_axis(x, index, axis=axis, mode="promise_in_bounds")

def turn(x, sign):
    row, lane = iota((8, 128), 0), iota((8, 128), 1)
    return take(x, (lane - sign * 32 * (row & 3)) & 127, 1)

def skew(x):
    row, chunk = iota((8, 128), 0), iota((8, 128), 1) >> 5
    return take(x, (row & 4) | ((chunk - row) & 3), 0)

def swap_chunks(x):
    return turn(skew(turn(x, 1)), -1)

def to_blocks(x):
    z = [swap_chunks(x[:, 128 * j:128 * j + 128]) for j in range(8)]
    low = iota((8, 128), 0) < 4
    left = [jnp.where(low, z[2 * i], pltpu.roll(z[2 * i + 1], 4, 0)) for i in range(4)]
    right = [jnp.where(low, pltpu.roll(z[2 * i], 4, 0), z[2 * i + 1]) for i in range(4)]
    return jnp.concatenate([jnp.concatenate(left, 0), jnp.concatenate(right, 0)], 1)

def from_blocks(y):
    low = iota((8, 128), 0) < 4
    out = []
    for i in range(4):
        l, r = y[8 * i:8 * i + 8, :128], y[8 * i:8 * i + 8, 128:]
        for z in (jnp.where(low, l, pltpu.roll(r, 4, 0)), jnp.where(low, pltpu.roll(l, 4, 0), r)):
            out.append(swap_chunks(z))
    return jnp.concatenate(out, 1)

def diagonal(y, half):
    part = y[:, 128 * half:128 * half + 128]
    chunk = iota(part.shape, 1) >> 5
    return jnp.concatenate([jnp.where(chunk == c, part, jnp.zeros_like(part)) for c in range(4)], 0)

def dot(a, b, dims=((1,), (0,))):
    return lax.dot_general(a, b, (dims, ((), ())), preferred_element_type=f32)

def two(parts): return jnp.concatenate(parts, 1)

def shift(x, k, back):
    n = 128 - k if back else k
    return two([pltpu.roll(x[:, :128], n, 1), pltpu.roll(x[:, 128:], n, 1)])

def spread(x3):
    r = ((iota((24, 256), 0) & 7) == (iota((24, 256), 1) >> 5)).astype(f32).astype(bf16)
    return dot(x3, r, ((0,), (0,)))

def roll_halves(x, amount, **kw):
    return two([pltpu.roll(x[:, :128], amount, 1, **kw), pltpu.roll(x[:, 128:], amount, 1, **kw)])

def lag_rows(row, amount):
    row = roll_halves(jnp.broadcast_to(row, (8, 256)), amount)
    return roll_halves(jnp.concatenate([row] * 4, 0), 0, stride=1, stride_axis=0)

def gelu_parts(x):
    k = 0.7978845608028654
    t = jnp.tanh(k * (x + 0.044715 * (x * x * x)))
    return t, k

def gelu(x):
    t, k = gelu_parts(x)
    return 0.5 * x * (1.0 + t)

def gelu_grad(x):
    t, k = gelu_parts(x)
    return 0.5 * (1.0 + t) + 0.5 * x * (1.0 - t * t) * k * (1.0 + 3 * 0.044715 * x * x)

def halved(x):
    hi = x.astype(bf16)
    return hi, (x - hi.astype(f32)).astype(bf16)

def each(f, *lists):
    return [f(*items) for items in zip(*lists)]

def scans(es, fs, mask_ref, first, back):
    for i in range(4):
        moved = each(lambda e: shift(e, 1 << i, back), es)
        m = mask_ref[first + i:first + i + 1, :]
        es = each(lambda e, f, s: e + (f * m) * s, es, fs, moved)
        if i < 3: fs = each(lambda f: f * f, fs)
    return es

def halves_dot(lhs, rights, width):
    return two([dot(lhs[:, width * h:width * h + width], rights[h]) for h in range(2)])

def fwd_groups(rev, xs, d3s, w3s, drows, wrows, skips, masks):
    vs = each(gelu, xs)
    vys = each(lambda v: to_blocks(v).astype(bf16), vs)
    d1s, w1s = each(spread, d3s), each(spread, w3s)
    pos = iota((64, 256), 1) & 31
    p = (pos if rev else 31 - pos).astype(f32)
    pts = each(lambda d1: jnp.exp(p * d1), d1s)
    krows = each(lambda w1, pt: jnp.sum(w1 * pt, axis=0, keepdims=True), w1s, pts)
    row, lane = iota((T, 256), 0), iota((T, 256), 1) & 31
    valid = (lane >= row if rev else row >= lane)
    toeps = each(lambda k: jnp.where(valid, lag_rows(k, 0 if rev else 97), 0.0), krows)
    lhss = each(lambda pt, t: jnp.concatenate([pt, t], 0).astype(bf16), pts, toeps)
    boths = each(lambda lhs, vy: halves_dot(lhs, [diagonal(vy, h) for h in range(2)], 128), lhss, vys)
    fs = each(lambda d1: jnp.exp(float(T) * d1), d1s)
    hs = scans([b[:64] for b in boths], fs, masks, 0, rev)
    hes = each(lambda h: masks[0:1, :] * shift(h, 1, rev), hs)
    col = iota((T, 512), 0)
    q = (T - col if rev else col + 1).astype(f32)
    leads = each(lambda wrow, drow: (wrow * jnp.exp(q * drow)).astype(bf16), wrows, drows)
    outers = each(lambda lead, he: halves_dot(lead, [diagonal(he.astype(bf16), h) for h in range(2)], 256), leads, hes)
    return each(lambda b, o, skip, v: from_blocks(b[64:] + o) + skip * v, boths, outers, skips, vs), hes

def fwd_kernel(groups, unroll, dir_ref, x_ref, d3_ref, w3_ref, drow_ref, wrow_ref, skip_ref, mask_ref, out_ref, enter_ref):
    def body(rev, i, _):
        gs = [i * unroll + u for u in range(unroll)]
        rows = [pl.ds(pl.multiple_of(g * 8, 8), 8) for g in gs]
        pick = lambda ref, at: [ref[a] for a in at]
        pickr = lambda ref: [ref[r, :] for r in rows]
        pickf = lambda ref: [ref[pl.ds(g, 1), :] for g in gs]
        outs, enters = fwd_groups(rev, pickr(x_ref), pick(d3_ref, gs), pick(w3_ref, gs), pickf(drow_ref), pickf(wrow_ref), pickr(skip_ref), mask_ref)
        for g, r, o, e in zip(gs, rows, outs, enters):
            out_ref[r, :] = o
            enter_ref[g] = e
        return 0
    for rev in (False, True):
        @pl.when(dir_ref[0] == int(rev))
        def _(rev=rev):
            lax.fori_loop(0, groups // unroll, functools.partial(body, rev), 0)

def flip_rows(y):
    row = iota((8, 128), 0)
    tiles = [[take(y[8 * i : 8 * i + 8, 128 * h : 128 * h + 128], 7 - row, 0) for h in range(2)] for i in (3, 2, 1, 0)]
    return jnp.concatenate([two(t) for t in tiles], 0)

def bwd_groups(rev, at_group, xs, gms, hes, d3s, w3s, drows, skips, masks):
    vs = each(gelu, xs)
    vys = each(lambda v: to_blocks(v).astype(bf16), vs)
    gfs = each(to_blocks, gms)
    gys = each(lambda g: g.astype(bf16), gfs)
    gyrs = each(lambda g: flip_rows(g).astype(bf16), gfs)
    d1s, w1s = each(spread, d3s), each(spread, w3s)
    pos = iota((64, 256), 1) & 31
    p = (pos if rev else 31 - pos).astype(f32)
    pts = each(lambda d1: jnp.exp(p * d1), d1s)
    ppts = each(lambda pt: p * pt, pts)
    rs = each(lambda d1: jnp.exp((31.0 - p) * d1), d1s)
    ats = each(lambda r, d1: r * jnp.exp(d1), rs, d1s)
    apts = each(lambda at: (32.0 - p) * at, ats)
    krows = each(lambda w1, r: jnp.sum(w1 * r, axis=0, keepdims=True), w1s, rs)
    row, lane = iota((T, 256), 0), iota((T, 256), 1) & 31
    ok2 = (row >= lane if rev else lane >= row)
    toeps = each(lambda k: jnp.where(ok2, lag_rows(k, 97 if rev else 0), 0.0), krows)
    lhs_v = each(lambda ppt: ppt.astype(bf16), ppts)
    lhs_g = each(lambda at, apt, t: jnp.concatenate([at, apt, t], 0).astype(bf16), ats, apts, toeps)
    bdvs = each(lambda vy: [diagonal(vy, h) for h in range(2)], vys)
    bdgs = each(lambda gy: [diagonal(gy, h) for h in range(2)], gys)
    ees = each(lambda l, b: halves_dot(l, b, 128), lhs_v, bdvs)
    qqs = each(lambda l, b: halves_dot(l, b, 128), lhs_g, bdgs)
    ms = each(lambda gy, b: two([dot(gy[:, 128 * h:128 * h + 128], b[h], ((1,), (1,))) for h in range(2)]), gyrs, bdvs)
    fs = each(lambda d1: jnp.exp(float(T) * d1), d1s)
    n = len(xs)
    downs = scans(each(lambda w1, q: w1 * q[:64], w1s, qqs), fs, masks, 4, not rev)
    des = each(lambda h: masks[4:5, :] * shift(h, 1, not rev), downs)
    col = iota((T, 512), 0)
    pw = (col if rev else 31 - col).astype(f32)
    p2s = each(lambda drow: jnp.exp(pw * drow).astype(bf16), drows)
    dvs = each(lambda qq, p2, de: qq[128:] + halves_dot(p2, [diagonal(de.astype(bf16), h) for h in range(2)], 256), qqs, p2s, des)
    ok = (lane + row >= 31 if rev else lane + row <= 31)
    ms = each(lambda m: roll_halves(jnp.where(ok, m, 0.0), 0, stride=1, stride_axis=0), ms)
    dks = each(lambda m: jnp.sum(m, axis=0, keepdims=True), ms)
    if rev: dks = each(lambda dk: roll_halves(jnp.broadcast_to(dk, (8, 256)), 97)[:1], dks)
    zws = each(lambda he, qq, pt, dk: he * qq[:64] + pt * dk, hes, qqs, pts, dks)
    zds = each(lambda w1, he, qq, ppt, dk, de, ee, f: w1 * (he * qq[64:128] + ppt * dk) + de * (ee + float(T) * f * he), w1s, hes, qqs, ppts, dks, des, ees, fs)
    total = 0.0
    for u, (zw, zd) in enumerate(zip(zws, zds)):
        column = 8 * (at_group + u) + (iota((256, 128), 0) >> 5)
        ones = (iota((256, 128), 1) == column).astype(f32).astype(bf16)
        both = dot(jnp.concatenate([*halved(zw), *halved(zd)], 0), ones)
        total = total + jnp.concatenate([both[:64] + both[64:128], both[128:192] + both[192:]], 0)
    dvals = each(lambda dv, skip, gm, x: (from_blocks(dv) + skip * gm) * gelu_grad(x), dvs, skips, gms, xs)
    dskips = each(lambda gm, v: jnp.sum(gm * v, axis=1, keepdims=True), gms, vs)
    return dvals, total, dskips

def bwd_kernel(groups, unroll, dir_ref, x_ref, gm_ref, enter_ref, d3_ref, w3_ref, drow_ref, skip_ref, mask_ref, gv_ref, grads_ref, dskip_ref, dbias_ref):
    grads_ref[...] = jnp.zeros_like(grads_ref)
    def body(rev, i, _):
        gs = [i * unroll + u for u in range(unroll)]
        rows = [pl.ds(pl.multiple_of(g * 8, 8), 8) for g in gs]
        pick = lambda ref: [ref[a] for a in gs]
        pickr = lambda ref: [ref[r, :] for r in rows]
        pickf = lambda ref: [ref[pl.ds(g, 1), :] for g in gs]
        gms = pickr(gm_ref)
        dvals, total, dskips = bwd_groups(rev, i * unroll, pickr(x_ref), gms, pick(enter_ref), pick(d3_ref), pick(w3_ref), pickf(drow_ref), pickr(skip_ref), mask_ref)
        grads_ref[...] += total
        for r, a, c in zip(rows, dvals, dskips):
            dskip_ref[r, :] = c
            dbias_ref[r, :] = jnp.sum(a.astype(bf16).astype(f32), axis=1, keepdims=True)
        for u in range(0, unroll, 2):
            gv_ref[pl.ds(pl.multiple_of((i * unroll + u) * 8, 16), 16), :] = jnp.concatenate(dvals[u : u + 2], 0).astype(bf16)
        return 0
    for rev in (False, True):
        @pl.when(dir_ref[0] == int(rev))
        def _(rev=rev):
            lax.fori_loop(0, groups // unroll, functools.partial(body, rev), 0)

def specs(cb, first):
    g = cb // 8
    rows = lambda lanes: pl.BlockSpec((cb, lanes), lambda i: (i + first, 0))
    per = lambda a, b: pl.BlockSpec((g, a, b), lambda i: (i + first, 0, 0))
    flat = lambda lanes: pl.BlockSpec((g, lanes), lambda i: (i + first, 0))
    return rows, per, flat

def mix_call(kernel, name, out_shape, in_specs, out_specs, steps, done, args):
    n = len(args)
    if done is None:
        body, aliases, done = kernel, {}, ()
    else:
        body = lambda *refs: kernel(*refs[:n], *refs[n + len(done):])
        aliases = {n + i: i for i in range(len(done))}
        in_specs = in_specs + [pl.BlockSpec(memory_space=pl.ANY)] * len(done)
    return pl.pallas_call(
        body,
        out_shape=out_shape,
        grid=(steps,),
        in_specs=in_specs,
        out_specs=out_specs,
        input_output_aliases=aliases,
        compiler_params=pltpu.CompilerParams(vmem_limit_bytes=60 << 20),
        name=name,
    )(*args, *done)

MASKS = pl.BlockSpec((8, 256), lambda i: (0, 0))
SCALAR = pl.BlockSpec(memory_space=pltpu.SMEM)

def ssm_fwd(direction, x, d3, w3, drow, wrow, skip, masks, part=0, parts=1, done=None, cb=64, unroll=8):
    c, tok = x.shape
    steps = c // cb // parts
    rows, per, flat = specs(cb, part * steps)
    return mix_call(
        functools.partial(fwd_kernel, cb // 8, unroll),
        f"mix_forward_{part}",
        (jax.ShapeDtypeStruct((c, tok), f32), jax.ShapeDtypeStruct((c // 8, 64, 256), f32)),
        [SCALAR, rows(tok), per(24, 64), per(24, 64), flat(512), flat(512), rows(1), MASKS],
        (rows(tok), per(64, 256)),
        steps, done, (direction, x, d3, w3, drow, wrow, skip, masks),
    )

def ssm_bwd(direction, x, gm, enter, d3, w3, drow, skip, masks, part=0, parts=1, done=None, cb=128, unroll=8):
    c, tok = x.shape
    steps = c // cb // parts
    first = part * steps
    rows, per, flat = specs(cb, first)
    return mix_call(
        functools.partial(bwd_kernel, cb // 8, unroll),
        f"mix_backward_{part}",
        (jax.ShapeDtypeStruct((c, tok), bf16), jax.ShapeDtypeStruct((128, c), f32), jax.ShapeDtypeStruct((c, 1), f32), jax.ShapeDtypeStruct((c, 1), f32)),
        [SCALAR, rows(tok), rows(tok), per(64, 256), per(24, 64), per(24, 64), flat(512), rows(1), MASKS],
        (rows(tok), pl.BlockSpec((128, cb), lambda i: (0, i + first)), rows(1), rows(1)),
        steps, done, (direction, x, gm, enter, d3, w3, drow, skip, masks),
    )

def thirds(x):
    hi = x.astype(bf16)
    rest = x - hi.astype(f32)
    mid = rest.astype(bf16)
    lo = (rest - mid.astype(f32)).astype(bf16)
    c = x.shape[0]
    return jnp.concatenate([a.reshape(c // 8, 8, 64) for a in (hi, mid, lo)], 1)

def block_masks(labels, rev):
    idx = jnp.arange(16)[None, :]
    def reach(k, back):
        other = jnp.roll(labels, -k if back else k, axis=1)
        inside = (idx + k < 16) if back else (idx >= k)
        return (inside & (other == labels)).astype(f32).reshape(32)
    ahead = jnp.stack([reach(k, False) for k in (1, 2, 4, 8)])
    behind = jnp.stack([reach(k, True) for k in (1, 2, 4, 8)])
    both = jnp.where(rev, jnp.concatenate([behind, ahead]), jnp.concatenate([ahead, behind]))
    return jnp.tile(both, (1, 8))


ROUNDS = (
    {"x": "own", "y": "own", "z": "own", "o": "own", "m": "own"},
    {"x": (0, "y"), "y": (0, "z"), "z": (0, "m"), "o": (0, "x"), "m": (0, "z")},
    {"x": (1, "y"), "y": (1, "z"), "z": (1, "m"), "o": (1, "z"), "m": (1, "y")},
    {"x": (2, "z"), "y": (2, "z"), "z": (0, "x"), "o": (0, "x"), "m": (2, "x")},
    {"x": (2, "y"), "y": (3, "x"), "z": (3, "x"), "o": (3, "x")},
)
PERMS = {
    "x": [(w, w ^ 1) for w in range(16)],
    "y": [(w, w ^ 2) for w in range(16)],
    "z": [(w, w ^ 4) for w in range(16)],
    "m": [(w, w + 4) for w in range(4, 8)] + [(w, w - 4) for w in range(8, 12)],
}


def trace_rounds():
    end, mid = {"own": (0, 0, 0)}, {"own": (0, 0, 1)}
    for r, sends in enumerate(ROUNDS):
        new_end, new_mid = {}, {}
        for d, bit in (("x", 0), ("y", 1)):
            for held, new in ((end, new_end), (mid, new_mid)):
                item = list(held[sends[d]])
                item[bit] ^= 1
                new[(r, d)] = tuple(item)
        new_end[(r, "z")], new_mid[(r, "z")] = mid[sends["z"]], end[sends["o"]]
        if "m" in sends:
            dx, dy, layer = mid[sends["m"]]
            new_end[(r, "m")], new_mid[(r, "m")] = None, (dx, dy, 3 - layer)
        end.update(new_end)
        mid.update(new_mid)

    def firsts(held):
        seen, first = set(), {}
        for slot, item in held.items():
            first[slot] = item is not None and item not in seen
            seen.add(item)
        return first

    return end, mid, firsts(end), firsts(mid)


END, MID, FIRST_END, FIRST_MID = trace_rounds()
SLOTS = tuple(END)


def at_end():
    layer = lax.axis_index("wide") >> 2
    return (layer == 0) | (layer == 3)


def owner(slot):
    w = lax.axis_index("wide")
    x, y, layer = w & 1, (w >> 1) & 1, w >> 2

    def of(held):
        dx, dy, z = held[slot] or (0, 0, 0)
        return jnp.where(layer >= 2, 3 - z, z) * 4 + (y ^ dy) * 2 + (x ^ dx)

    return jnp.where(at_end(), of(END), of(MID))


def is_first(slot):
    return jnp.where(at_end(), int(FIRST_END[slot]), int(FIRST_MID[slot]))


def core_index():
    return lax.axis_index("narrow") & 1


def within_half(w, rows):
    return pl.multiple_of((w & 7) * rows, 16)


ANY = pl.BlockSpec(memory_space=pl.ANY)
HBM = pl.BlockSpec(memory_space=pltpu.HBM)
VM = pl.BlockSpec(memory_space=pltpu.VMEM)


def params(mib=60):
    return pltpu.CompilerParams(vmem_limit_bytes=mib << 20)


def shape(dims, dtype):
    return jax.ShapeDtypeStruct(dims, dtype)


def ones_where(condition):
    return jnp.where(condition, 1.0, 0.0).astype(bf16)


def pack_kernel(up, value, proj, out, rate, in_map, out_map, *refs):
    *vectors, keep, send, rows = refs
    def lanes(n, first):
        return ones_where(iota((n, 256), 1) == iota((n, 256), 0) + first)

    rows[...] = jnp.zeros((16, 48), f32)
    k = 0
    for ref in vectors:
        v = ref[...].astype(f32)
        for first in range(0, v.shape[0], 48):
            part = v[first : first + 48]
            rows[k, : part.shape[0]] = part
            k += 1
    small = dot(rows[...].astype(bf16), lanes(16, 192), ((0,), (0,)))
    for k, ref in enumerate((rate, in_map, out_map)):
        small = small + dot(ref[...], lanes(64, 64 * k))
    for core in range(2):

        @pl.when(core_index() == core)
        def _(core=core):
            for ref, half in ((keep, core), (send, 1 - core)):
                a = up[...].astype(f32)
                for q in range(2):
                    ref[24 * q : 24 * q + 24, :] = a[:, 1536 * half + 768 * q : 1536 * half + 768 * q + 768]
                ref[48:72, :] = value[...].astype(f32)[:, 768 * half : 768 * half + 768]
                ref[72:168, :] = proj[...].astype(f32)[:, 768 * half : 768 * half + 768]
                b = out[...].astype(f32)[:, 384 * half : 384 * half + 384]
                ref[168:192, :384] = b[:24]
                ref[168:192, 384:] = b[24:]
                for j in range(3):
                    ref[192:208, 256 * j : 256 * j + 256] = small[16 * j : 16 * j + 16, :]


def pack(*shards):
    return pl.pallas_call(
        pack_kernel,
        out_shape=(shape((208, 768), f32),) * 2,
        in_specs=[VM] * len(shards),
        out_specs=(VM, VM),
        scratch_shapes=[pltpu.VMEM((16, 48), f32)],
        compiler_params=params(),
        name="pack_shards",
    )(*shards)


def merge_kernel(keep, recv, blob):
    for core in range(2):

        @pl.when(core_index() == core)
        def _(core=core):
            lo, hi = (keep, recv) if core == 0 else (recv, keep)

            def both(a, n):
                return jnp.concatenate([lo[a : a + n, :], hi[a : a + n, :]], 0)

            for q in range(2):
                blob[48 * q : 48 * q + 48, :] = both(24 * q, 24).astype(bf16)
            blob[96:144, :] = both(48, 24).astype(bf16)
            s = [ref[192:208, 256 * j : 256 * j + 256] for ref in (lo, hi) for j in range(3)]
            for j in range(3):
                blob[144:176, 256 * j : 256 * j + 256] = jnp.concatenate(s[2 * j : 2 * j + 2], 0).astype(bf16)
            blob[176:368, :] = both(72, 96).astype(bf16)
            for k, ref in enumerate((lo, hi)):
                rows = jnp.concatenate([ref[168:192, :384], ref[168:192, 384:]], 0)
                blob[368:416, 384 * k : 384 * k + 384] = rows.astype(bf16)


def merge(keep, recv):
    return pl.pallas_call(
        merge_kernel,
        out_shape=shape((416, 768), bf16),
        in_specs=[VM, VM],
        out_specs=VM,
        compiler_params=params(),
        name="merge_pair",
    )(keep, recv)


def together(*trees):
    return lax.optimization_barrier(trees)


def gather_rounds(own, work, state=None):
    held = {"own": own}
    end = at_end()
    for r, sends in enumerate(ROUNDS):
        blocks = {}
        for d in "xyzm":
            if d in sends:
                block = held[sends[d]]
                if d == "z" and sends["z"] != sends["o"]:
                    block = jnp.where(end, held[sends["o"]], block)
                blocks[d] = block
        blocks, state = together(blocks, state)
        came = {d: lax.ppermute(block, "wide", PERMS[d]) for d, block in blocks.items()}
        state = work[r](state)
        if r == len(ROUNDS) - 1:
            early = dict(held)
            early[sends["x"]] = blocks["x"]
            placed = place_all(tuple(early), tuple(early.values()))
            came, placed, state = together(came, placed, state)
            late = {(r, d): block for d, block in came.items()}
            return place_all(tuple(late), tuple(late.values()), placed), state
        came, state = together(came, state)
        held.update({(r, d): block for d, block in came.items()})


def place_kernel(slots, pieces, outs, held, *refs):
    n = len(slots)
    blocks, refs = refs[:n], refs[n + held :]
    dests, (buf, in_sem, out_sem) = refs[:outs], refs[outs:]

    def each_slot(act):
        for i, slot in enumerate(slots):
            if FIRST_END[slot] and FIRST_MID[slot]:
                act(i, owner(slot))
            else:
                pl.when(is_first(slot) == 1)(functools.partial(act, i, owner(slot)))

    def load(i):
        return pltpu.make_async_copy(blocks[i], buf.at[i], in_sem.at[i])

    def stores(i, w):
        mine = (w >> 3) == core_index()
        for src, which, dst in pieces:

            def go(at, src=src, dst=dst):
                pltpu.make_async_copy(buf.at[(i,) + src], dests[at].at[dst(w)], out_sem.at[i]).start()

            if isinstance(which, int):
                go(which)
            else:
                pl.when(mine)(functools.partial(go, which[0]))
                pl.when(jnp.logical_not(mine))(functools.partial(go, which[1]))

    def load_start(i, w):
        load(i).start()

    def pass_on(i, w):
        load(i).wait()
        stores(i, w)

    def finish(i, w):
        pltpu.make_async_copy(blocks[i], buf.at[i], out_sem.at[i]).wait()

    for act in (load_start, pass_on, finish):
        each_slot(act)


def place(slots, blocks, pieces, out_shapes, done, name):
    n, held = len(slots), len(done)
    return pl.pallas_call(
        functools.partial(place_kernel, slots, pieces, len(out_shapes), held),
        out_shape=out_shapes,
        in_specs=[ANY] * (n + held),
        out_specs=tuple(ANY for _ in out_shapes),
        input_output_aliases={n + k: k for k in range(held)},
        scratch_shapes=[
            pltpu.VMEM((n,) + blocks[0].shape, bf16),
            pltpu.SemaphoreType.DMA((n,)),
            pltpu.SemaphoreType.DMA((n,)),
        ],
        compiler_params=params(),
        name=name,
    )(*blocks, *done)


def place_all(slots, blocks, done=()):
    full = slice(None)
    pieces = [
        ((slice(0, 48), full), 0, lambda w: (pl.ds(pl.multiple_of(w * 48, 16), 48), slice(0, 768))),
        ((slice(48, 96), full), 0, lambda w: (pl.ds(pl.multiple_of(w * 48, 16), 48), slice(768, 1536))),
        ((slice(96, 144), full), 1, lambda w: (pl.ds(pl.multiple_of(w * 48, 16), 48), full)),
        ((slice(176, 368), full), (3, 4), lambda w: (pl.ds(within_half(w, 192), 192), full)),
    ]
    for j in range(3):
        pieces.append(
            (
                (slice(144, 176), slice(256 * j, 256 * j + 256)),
                2,
                lambda w, j=j: (pl.ds(pl.multiple_of(w * 96 + 32 * j, 16), 32), full),
            )
        )
    for k in range(2):
        pieces.append(
            (
                (slice(368, 416), slice(384 * k, 384 * k + 384)),
                (5, 6),
                lambda w, k=k: (pl.ds(within_half(w, 96) + 48 * k, 48), full),
            )
        )
    dims = ((768, 1536), (768, 768), (1536, 256), (1536, 768), (1536, 768), (768, 384), (768, 384))
    name = "place_last" if done else "place_first"
    return place(slots, blocks, pieces, tuple(shape(d, bf16) for d in dims), done, name)


def divided_by_48(x):
    return (x * 1366) >> 16


def row_of_wide(shape_of, width_dim):
    d = iota(shape_of, width_dim)
    w = divided_by_48(d)
    rest = d - 48 * w
    c = jnp.where(rest >= 24, 1, 0)
    return 96 * w + 48 * c + rest - 24 * c


def row_of_up(shape_of, up_dim):
    f = iota(shape_of, up_dim)
    q = divided_by_48(f)
    return 96 * (q >> 2) + 48 * ((q >> 1) & 1) + f - 48 * q, q & 1


def mix_parameters(mine):
    rate = -jnp.exp(mine[:, :64])
    step = jnp.exp(mine[:, 192:193])
    decay_log = step * rate
    decay = jnp.exp(decay_log)
    gap = (decay - 1.0) / rate
    return rate, step, decay_log, decay, gap


def coefficients_kernel(table, labels, d3, w3, drow, wrow, skip, value_b, proj_b, up_b, wide, masks, buf):
    half = pl.ds(pl.multiple_of(core_index() * 768, 256), 768)
    mine = table[half, :].astype(f32)
    rate, step, decay_log, decay, gap = mix_parameters(mine)
    weight = mine[:, 128:192] * gap * mine[:, 64:128]
    for v, three, row in ((decay_log, d3, drow), (weight, w3, wrow)):
        parts, rest = [], v
        for _ in range(3):
            part = rest.astype(bf16).astype(f32)
            parts.append(part.reshape(96, 8, 64))
            rest = rest - part
        three[...] = jnp.concatenate(parts, 1).astype(bf16)
        buf[...] = v
        for c in range(8):
            row[:, 64 * c : 64 * c + 64] = buf[pl.ds(c, 96, stride=8), :]
    skip[...] = mine[:, 193:194]
    value_b[...] = mine[:, 194:195]
    low = table[half, 128:]
    proj_b[...] = mine[:, 128:].T[67:68, :]
    r, k = row_of_up((768, 1536), 1)
    at = r == iota((768, 1536), 0)
    pick = lambda which: dot(low, ones_where(at & (k == which)), ((0,), (0,)))
    up_b[...] = pick(0)[68:69, :] + pick(1)[69:70, :]
    spread_wide = ones_where(row_of_wide((1536, 768), 1) == iota((1536, 768), 0))
    wide[...] = dot(table[:, 128:], spread_wide, ((0,), (0,)))[70:73, :]
    lane = iota((8, 256), 1)
    each_lane = ones_where((iota((32, 256), 1) & 31) == iota((32, 256), 0))
    label = dot(jnp.broadcast_to(labels[...], (8, 32)).astype(bf16), each_lane)
    rows = []
    for k in (1, 2, 4, 8):
        before = jnp.where(((lane & 15) >= k) & (roll_halves(label, k) == label), 1.0, 0.0)
        behind = jnp.where(((lane & 15) + k < 16) & (roll_halves(label, 128 - k) == label), 1.0, 0.0)
        rows.append((before, behind))
    back = core_index() == 1
    for i, (before, behind) in enumerate(rows):
        masks[i : i + 1, :] = jnp.where(back, behind, before)[:1]
        masks[4 + i : 5 + i, :] = jnp.where(back, before, behind)[:1]


def coefficients(table, labels):
    dims = [((96, 24, 64), bf16)] * 2 + [((96, 512), f32)] * 2 + [((768, 1), f32)] * 2 + [((1, 768), f32), ((1, 1536), f32), ((3, 768), f32), ((8, 256), f32)]
    return pl.pallas_call(
        coefficients_kernel,
        out_shape=tuple(shape(*d) for d in dims),
        in_specs=[VM, VM],
        out_specs=(VM,) * len(dims),
        scratch_shapes=[pltpu.VMEM((768, 64), f32)],
        compiler_params=params(),
        name="coefficients",
    )(table, labels)


def small_sums_kernel(table, grads, skip, value_b, proj_b, up_b, gain, shift, out_b, out, buf, turn_buf):
    half = pl.ds(pl.multiple_of(core_index() * 768, 256), 768)
    theirs = pl.ds(pl.multiple_of((1 - core_index()) * 768, 256), 768)
    mine = table[half, :].astype(f32)
    rate, step, decay_log, decay, gap = mix_parameters(mine)
    in_p, out_p = mine[:, 64:128], mine[:, 128:192]
    both = grads[...].T
    weight, slope = both[:, :64], both[:, 64:]
    product = out_p * in_p
    through = slope * decay_log
    buf[theirs, :] = jnp.zeros((768, 256), f32)
    buf[half, 128:] = jnp.zeros((768, 128), f32)
    turn_buf[...] = jnp.zeros((128, 128), f32)
    buf[half, 0:64] = through + weight * (product * (decay * step - gap))
    buf[half, 64:128] = weight * out_p * gap
    buf[half, 128:192] = weight * in_p * gap
    buf[half, 192:193] = jnp.sum(through + weight * (product * decay * step), axis=1, keepdims=True)
    for k, ref in enumerate((skip, value_b)):
        buf[half, 193 + k : 194 + k] = ref[...]
    buf[half, 195:196] = jnp.broadcast_to(proj_b[...], (8, 768)).T[:, :1]
    for q in range(32):
        turn_buf[q : q + 1, 0:48] = up_b[:, 48 * q : 48 * q + 48]
        for k, ref in enumerate((gain, shift, out_b)):
            turn_buf[32 + 3 * q + k : 33 + 3 * q + k, 0:24] = ref[:, 24 * q : 24 * q + 24]
    columns = turn_buf[...].T
    for q in range(16):
        buf[pl.ds(pl.multiple_of(core_index() * 768 + 48 * q, 16), 48), 196:198] = columns[:48, 2 * q : 2 * q + 2]
    for q in range(32):
        buf[48 * q : 48 * q + 24, 198:201] = columns[:24, 32 + 3 * q : 35 + 3 * q]
    for w in range(16):
        for j in range(3):
            out[w, :, 256 * j : 256 * j + 256] = buf[96 * w + 32 * j : 96 * w + 32 * j + 32, :]


def small_sums(*args):
    return pl.pallas_call(
        small_sums_kernel,
        out_shape=shape((16, 32, 768), f32),
        in_specs=[VM] * len(args),
        out_specs=VM,
        scratch_shapes=[pltpu.VMEM((1536, 256), f32), pltpu.VMEM((128, 128), f32)],
        compiler_params=params(),
        name="small_sums",
    )(*args)


def children_of():
    kids = {s: [] for s in SLOTS}
    for r, sends in enumerate(ROUNDS):
        for d in "xyzm":
            if d not in sends:
                continue
            if d != "z" or sends["z"] == sends["o"]:
                kids[sends[d]].append(((r, d), None))
            else:
                kids[sends["z"]].append(((r, "z"), "mid"))
                kids[sends["o"]].append(((r, "z"), "end"))
    return kids


KIDS = children_of()


def sum_kernel(slots, pieces, n_own, arrived, rows, final, *refs):
    owns, refs = refs[:n_own], refs[n_own:]
    ins, refs = refs[: len(arrived)], refs[len(arrived) :]
    n_out = 2 if final else len(slots)
    outs, (own_buf, small_buf, in_buf, out_buf, own_sem, small_sem, in_sem, out_sem) = refs[:n_out], refs[n_out:]
    in_copies = []

    def start_own(p):
        w = owner(slots[p])
        mine = (w >> 3) == core_index()
        for choices, dst in pieces:
            for choice, (which, src) in enumerate(choices):

                def go(which=which, src=src, dst=dst):
                    buf, sem = (own_buf, own_sem) if owns[which].dtype == bf16 else (small_buf, small_sem)
                    pltpu.make_async_copy(owns[which].at[src(w)], buf.at[(p,) + dst], sem.at[p]).start()

                if len(choices) == 1:
                    go()
                else:
                    pl.when(mine == (choice == 0))(go)

    def wait_own(p):
        for buf, sem in ((own_buf, own_sem), (small_buf, small_sem)):
            pltpu.make_async_copy(buf.at[p], buf.at[p], sem.at[p]).wait()

    for p in range(len(slots)):
        start_own(p)
    for k in range(len(arrived)):
        in_copies.append(pltpu.make_async_copy(ins[k], in_buf.at[k], in_sem.at[k]))
        in_copies[-1].start()
    end = at_end()
    waited = set()
    sent = []
    for p, slot in enumerate(slots):
        wait_own(p)
        parts = []
        for kid, layers in KIDS[slot]:
            k = arrived.index(kid)
            if k not in waited:
                in_copies[k].wait()
                waited.add(k)
            parts.append((k, None if layers is None else jnp.where(end == (layers == "end"), 1.0, 0.0)))
        whole = FIRST_END[slot] and FIRST_MID[slot]
        keep = None if whole else is_first(slot).astype(f32)

        def add(i, _, p=p, parts=parts, keep=keep, own=own_buf, first=0):
            at = pl.ds(pl.multiple_of(i * 32, 32), 32)
            to = pl.ds(pl.multiple_of(first + i * 32, 32), 32)
            total = own[p, at, :].astype(f32)
            if keep is not None:
                total = total * keep
            for k, mask in parts:
                v = in_buf[k, to, :].astype(f32)
                total = total + (v if mask is None else v * mask)
            out_buf[p, to, :] = total.astype(out_buf.dtype)
            return 0

        low_rows, small_rows = own_buf.shape[1], small_buf.shape[1]
        lax.fori_loop(0, low_rows // 32, add, 0, unroll=4)
        lax.fori_loop(0, small_rows // 32, functools.partial(add, own=small_buf, first=low_rows), 0)
        if not final:
            sent.append(pltpu.make_async_copy(out_buf.at[p], outs[p], out_sem.at[p]))
            sent[-1].start()
    if final:
        for i, (ref, core) in enumerate(((outs[0], core_index()), (outs[1], 1 - core_index()))):
            for k, (src, dst) in enumerate(final):
                sent.append(pltpu.make_async_copy(out_buf.at[(0,) + src(core)], ref.at[dst], out_sem.at[i * len(final) + k]))
                sent[-1].start()
    for c in sent:
        c.wait()


def sum_slots(slots, owns, pieces, came, rows, final=None, final_rows=None, name="sum"):
    arrived = []
    for slot in slots:
        for kid, _ in KIDS[slot]:
            if kid not in arrived:
                arrived.append(kid)
    if final:
        out_shapes = (shape((final_rows, 768), f32),) * 2
    else:
        out_shapes = tuple(shape((rows, 768), bf16) for _ in slots)
    return pl.pallas_call(
        functools.partial(sum_kernel, slots, pieces, len(owns), arrived, rows, final),
        out_shape=out_shapes,
        in_specs=[ANY] * (len(owns) + len(arrived)),
        out_specs=tuple(HBM for _ in out_shapes),
        scratch_shapes=[
            pltpu.VMEM((len(slots), rows - 32, 768), bf16),
            pltpu.VMEM((len(slots), 32, 768), f32),
            pltpu.VMEM((max(1, len(arrived)), rows, 768), bf16),
            pltpu.VMEM((len(slots), rows, 768), f32 if final else bf16),
            pltpu.SemaphoreType.DMA((len(slots),)),
            pltpu.SemaphoreType.DMA((len(slots),)),
            pltpu.SemaphoreType.DMA((max(1, len(arrived)),)),
            pltpu.SemaphoreType.DMA((2 * len(final) if final else len(slots),)),
        ],
        compiler_params=params(),
        name=name,
    )(*owns, *[came[k] for k in arrived])


def scatter_rounds(owns, pieces, rows, final, final_rows, name, work, state=None):
    came = {}
    for r in reversed(range(len(ROUNDS))):
        slots = [(r, d) for d in "xyzm" if d in ROUNDS[r]]
        blocks = sum_slots(slots, owns, pieces, came, rows, name=f"{name}_{r}")
        blocks, state = together(blocks, state)
        new = {slot: lax.ppermute(block, "wide", PERMS[slot[1]]) for slot, block in zip(slots, blocks)}
        state = work[len(ROUNDS) - 1 - r](state)
        new, state = together(new, state)
        came.update(new)
    return sum_slots(["own"], owns, pieces, came, rows, final, final_rows, name=f"{name}_own"), state


def scatter_all(proj_mine, proj_theirs, out, out_theirs, up, value, small, work, state):
    full = slice(None)

    pieces = [([(i, lambda w: (pl.ds(within_half(w, 192), 192), full)) for i in (0, 1)], (slice(0, 192), full))]
    for k in range(2):
        pieces.append(
            (
                [(i, lambda w, k=k: (pl.ds(within_half(w, 96) + 48 * k, 48), full)) for i in (2, 3)],
                (slice(192, 240), slice(384 * k, 384 * k + 384)),
            )
        )
        pieces.append(
            (
                [(4, lambda w, k=k: (pl.ds(pl.multiple_of(w * 48, 16), 48), slice(768 * k, 768 * k + 768)))],
                (slice(240 + 48 * k, 288 + 48 * k), full),
            )
        )
    pieces.append(([(5, lambda w: (pl.ds(pl.multiple_of(w * 48, 16), 48), full))], (slice(336, 384), full)))
    pieces.append(([(6, lambda w: (w,))], (slice(0, 32), full)))
    final = [
        (lambda c: (pl.ds(pl.multiple_of(c * 96, 8), 96), full), (slice(0, 96), full)),
        (lambda c: (slice(192, 240), pl.ds(pl.multiple_of(c * 384, 128), 384)), (slice(96, 144), slice(0, 384))),
        (lambda c: (slice(384, 416), full), (slice(216, 248), full)),
    ] + [
        (
            lambda c, q=q: (pl.ds(pl.multiple_of(240 + q * 48 + c * 24, 8), 24), full),
            (slice(144 + 24 * q, 168 + 24 * q), full),
        )
        for q in range(3)
    ]
    owns = (proj_mine, proj_theirs, out, out_theirs, up, value, small)
    return scatter_rounds(owns, pieces, 416, final, 248, "sum", work, state)


def unpack_kernel(mine, recv, proj, out, up, value, rate, in_map, out_map, *refs):
    *vectors, small = refs
    for core in range(2):

        @pl.when(core_index() == core)
        def _(core=core):
            for ref, half in ((mine, core), (recv, 1 - core)):
                proj[:, 768 * half : 768 * half + 768] = ref[:96, :]
                out[:, 384 * half : 384 * half + 384] = ref[96:144, :384]
                for q in range(2):
                    up[:, 1536 * half + 768 * q : 1536 * half + 768 * q + 768] = ref[144 + 24 * q : 168 + 24 * q, :]
                value[:, 768 * half : 768 * half + 768] = ref[192:216, :]
            s = mine[216:248, :] + recv[216:248, :]
            if core == 0:
                small[:32, :] = s[:, :256]
                small[32:, :] = s[:16, 256:512]
            else:
                small[:16, :] = s[16:, 256:512]
                small[16:, :] = s[:, 512:]

    rate[...] = small[:, :64]
    in_map[...] = small[:, 64:128]
    out_map[...] = small[:, 128:192]
    rows = small[:, 128:].T
    for k, ref in enumerate(vectors[:4] + vectors[5:]):
        row = 64 + k if k < 4 else 66 + k
        ref[...] = rows[row, : ref.shape[0]]
    vectors[4][0:48] = rows[68, :]
    vectors[4][48:96] = rows[69, :]


def unpack(mine, recv):
    dims = ((96, 1536), (48, 768), (24, 3072), (24, 1536), (48, 64), (48, 64), (48, 64)) + ((48,),) * 4 + ((96,), (24,), (24,), (24,))
    return pl.pallas_call(
        unpack_kernel,
        out_shape=tuple(shape(d, f32) for d in dims),
        in_specs=[VM, VM],
        out_specs=(VM,) * len(dims),
        scratch_shapes=[pltpu.VMEM((48, 256), f32)],
        compiler_params=params(),
        name="unpack_sums",
    )(mine, recv)


TILE = 256


def tokens_by(width):
    return pl.BlockSpec((TILE, width), lambda i: (i, 0))


def by_tokens(rows):
    return pl.BlockSpec((rows, TILE), lambda i: (0, i))


def whole_block(*dims):
    return pl.BlockSpec(dims, lambda i: (0,) * len(dims))


def enter_kernel(unit, wide, up_w, up_b, value_w, value_b, normed, up_pre, up_low, value_pre):
    low = (unit[...] * wide[0:1, :] + wide[1:2, :]).astype(bf16)
    normed[...] = low
    value_pre[...] = dot(low, value_w[...]).T + value_b[...]
    for k in range(0, up_w.shape[1], 512):
        at = slice(k, k + 512)
        pre = dot(low, up_w[:, at]) + up_b[:, at]
        up_pre[:, at] = pre
        up_low[:, at] = gelu(pre).astype(bf16)


def enter(unit, wide, up_w, up_b, value_w, value_b):
    n, d = unit.shape
    f, c = up_w.shape[1], value_w.shape[1]
    return pl.pallas_call(
        enter_kernel,
        out_shape=(shape((n, d), bf16), shape((n, f), f32), shape((n, f), bf16), shape((c, n), f32)),
        grid=(n // TILE,),
        in_specs=[tokens_by(d)] + [whole_block(*v.shape) for v in (wide, up_w, up_b, value_w, value_b)],
        out_specs=(tokens_by(d), tokens_by(f), tokens_by(f), by_tokens(c)),
        compiler_params=params(),
        name="enter",
    )(unit, wide, up_w, up_b, value_w, value_b)


def gate_kernel(up, up_other, g, mixed, proj_mine, proj_theirs, proj_b, out_a, out_b, gm, gated, gp, grad_b, grad_mine, grad_theirs, grad_out, grad_send, acc, acc_out, out_w):
    step, steps = pl.program_id(0), pl.num_programs(0)

    @pl.when(step == 0)
    def _():
        acc[...] = jnp.zeros_like(acc)
        acc_out[...] = jnp.zeros_like(acc_out)
        grad_b[...] = jnp.zeros_like(grad_b)
        for core in range(2):

            @pl.when(core_index() == core)
            def _(core=core):
                out_w[:, 384 * core : 384 * core + 384] = out_a[...]
                out_w[:, 384 - 384 * core : 768 - 384 * core] = out_b[...]

    proj = dot(up[...], proj_mine[...]) + dot(up_other[...], proj_theirs[...]) + proj_b[...]
    gg = dot(g[...], out_w[...], ((1,), (1,)))
    gm[...] = (gg * proj).T
    mix = mixed[...].T
    low = (mix * proj).astype(bf16)
    gated[...] = low
    gp_low = (gg * mix).astype(bf16)
    gp[...] = gp_low
    grad_b[...] += jnp.sum(gp_low.astype(f32), axis=0, keepdims=True)
    for k, ref in enumerate((up, up_other)):
        acc[k] += dot(ref[...], gp_low, ((0,), (0,)))
    acc_out[...] += dot(low, g[...], ((0,), (0,)))

    @pl.when(step == steps - 1)
    def _():
        grad_mine[...] = acc[0].astype(bf16)
        grad_theirs[...] = acc[1].astype(bf16)
        for core in range(2):

            @pl.when(core_index() == core)
            def _(core=core):
                grad_out[...] = acc_out[:, 384 * core : 384 * core + 384].astype(bf16)
                grad_send[...] = acc_out[:, 384 - 384 * core : 768 - 384 * core].astype(bf16)


def gate(up, up_other, g, mixed, proj_mine, proj_theirs, proj_b, out_a, out_b):
    n, f = up.shape
    c, d = out_a.shape[0], g.shape[1]
    return pl.pallas_call(
        gate_kernel,
        out_shape=(
            shape((c, n), f32),
            shape((n, c), bf16),
            shape((n, c), bf16),
            shape((1, c), f32),
            shape((f, c), bf16),
            shape((f, c), bf16),
            shape((c, d // 2), bf16),
            shape((c, d // 2), bf16),
        ),
        grid=(n // TILE,),
        in_specs=[tokens_by(f), tokens_by(f), tokens_by(d), by_tokens(c)]
        + [whole_block(*v.shape) for v in (proj_mine, proj_theirs, proj_b, out_a, out_b)],
        out_specs=(by_tokens(c), tokens_by(c), tokens_by(c), whole_block(1, c))
        + (whole_block(f, c), whole_block(f, c), whole_block(c, d // 2), whole_block(c, d // 2)),
        scratch_shapes=[pltpu.VMEM((2, f, c), f32), pltpu.VMEM((c, d), f32), pltpu.VMEM((c, d), bf16)],
        compiler_params=params(),
        name="gate",
    )(up, up_other, g, mixed, proj_mine, proj_theirs, proj_b, out_a, out_b)


def contract(left, right, left_dim, right_dim):
    return lax.dot_general(left, right, (((left_dim,), (right_dim,)), ((), ())), preferred_element_type=f32)


def by_core(core, zero, one):
    return jnp.where(core == 0, zero, one)


def in_order(core, mine, other, axis):
    return by_core(core, jnp.concatenate([mine, other], axis), jnp.concatenate([other, mine], axis))


def half_of(x, which, axis):
    size = x.shape[axis] // 2
    return lax.dynamic_slice_in_dim(x, which * size, size, axis)


def per_device(
    sizes,
    tokens,
    segment,
    cotangent,
    w_up,
    w_value,
    w_proj,
    w_out,
    norm_gain,
    norm_bias,
    bias_up,
    bias_value,
    bias_proj,
    bias_out,
    log_rate,
    log_step,
    input_map,
    output_map,
    skip_gain,
):
    both = ("wide", "narrow")
    core = core_index()
    pairs = [(i, i ^ 1) for i in range(sizes["narrow"])]
    staged = sizes["wide"] == 16 and sizes["narrow"] == 2

    def swap(x):
        return lax.ppermute(x, "narrow", pairs)

    tok, width = tokens.shape
    blocks = tok // T

    def by_place(x):
        return x.reshape(blocks, T, width).transpose(1, 0, 2)

    labels = segment.reshape(blocks, T)[:, 0].astype(f32)

    def whole_chip(mine, other):
        return by_core(core, jnp.stack([mine, other], 1), jnp.stack([other, mine], 1)).reshape(2 * tok, width)

    def normalise(x):
        x = x.astype(f32)
        average = jnp.mean(x, axis=-1, keepdims=True)
        centred = x - average
        scale = lax.rsqrt(jnp.mean(centred * centred, axis=-1, keepdims=True) + 1e-05)
        return centred * scale, scale

    if staged:
        vectors = (log_step, skip_gain, bias_value, bias_proj, bias_up, norm_gain, norm_bias, bias_out, labels)
        keep, send = pack(w_up, w_value, w_proj, w_out, log_rate, input_map, output_map, *vectors)
        recv = swap(send)
        other_labels = recv[192:208, 201]
        blob = merge(keep, recv)
        idle = lambda state: state

        def own_tokens(state):
            return jnp.stack([by_place(v) for v in state])

        def other_tokens(state):
            return state, swap(state)

        def chip_tokens(state):
            mine, theirs = state
            return mine, whole_chip(mine[0], theirs[0]), whole_chip(mine[1], theirs[1])

        def chip_unit(state):
            mine, x, g = state
            return mine, normalise(x)[0], g

        work = [own_tokens, other_tokens, chip_tokens, chip_unit, idle]
        placed, ((own_x, own_g), unit_chip, g_chip) = gather_rounds(blob, work, (tokens, cotangent))
        up_w, value_w, table, proj_mine, proj_theirs, out_mine, out_theirs = placed
        proj_cross = swap(proj_theirs)
        out_cross = swap(out_theirs)
        out_w = in_order(core, out_mine, out_cross, 1)
        label_row = in_order(core, labels, other_labels, 0)[None]
        coefs = coefficients(table, label_row)
        decay3, weight3, decay_row, weight_row, skip_p, value_b, proj_b, up_b, wide, masks = coefs
    else:
        own_x, own_g = by_place(tokens), by_place(cotangent)
        other_x, other_g = swap(own_x), swap(own_g)
        unit_chip, g_chip = normalise(whole_chip(own_x, other_x))[0], whole_chip(own_g, other_g)
        other_labels = swap(labels)
        whole = lambda p: lax.all_gather(p, both, axis=0, tiled=True)
        up_w = half_of(whole(w_up), core, 1)
        value_w = half_of(whole(w_value), core, 1)
        full = whole(w_proj)
        proj_mine = half_of(half_of(full, core, 1), core, 0)
        proj_theirs = half_of(half_of(full, core, 1), 1 - core, 0)
        proj_cross = half_of(half_of(full, 1 - core, 1), core, 0)
        out_w = half_of(whole(w_out), core, 0)
        out_mine, out_cross = half_of(out_w, core, 1), half_of(out_w, 1 - core, 1)
        rate_p, in_p, out_p = (half_of(whole(p).astype(f32), core, 0) for p in (log_rate, input_map, output_map))
        step_p, skip_p, value_b, proj_b = (
            half_of(whole(p).astype(f32), core, 0)[:, None] for p in (log_step, skip_gain, bias_value, bias_proj)
        )
        proj_b = proj_b.T
        up_b = half_of(whole(bias_up).astype(f32), core, 0)[None]
        wide = jnp.stack([whole(p).astype(f32) for p in (norm_gain, norm_bias, bias_out)])

    direction = core.astype(jnp.int32).reshape(1)
    if not staged:
        rate = -jnp.exp(rate_p)
        step = jnp.exp(step_p)
        decay_log = step * rate
        decay = jnp.exp(decay_log)
        gap = (decay - 1.0) / rate
        weight = out_p * gap * in_p
        masks = block_masks(in_order(core, labels[None], other_labels[None], 0), core == 1)
        decay_row, weight_row = (v.reshape(-1, 512) for v in (decay_log, weight))
        decay3, weight3 = thirds(decay_log), thirds(weight)
    normed_low, up_pre, up_low, value_pre = enter(unit_chip, wide, up_w, up_b, value_w, value_b)
    up_other = swap(up_low)
    mixed, entering = ssm_fwd(direction, value_pre, decay3, weight3, decay_row, weight_row, skip_p, masks)
    grad_mixed, gated_low, grad_proj_low, grad_proj_b, grad_proj_mine, grad_proj_theirs, grad_out_mine, grad_out_send = gate(
        up_low, up_other, g_chip, mixed, proj_mine, proj_theirs, proj_b, out_mine, out_cross
    )

    grad_proj_other = swap(grad_proj_low)
    grad_value_low, grad_mix, grad_skip, grad_value_b = ssm_bwd(
        direction, value_pre, grad_mixed, entering, decay3, weight3, decay_row, skip_p, masks
    )
    grad_up_act = contract(grad_proj_low, proj_mine, 1, 1) + contract(grad_proj_other, proj_cross, 1, 1)
    grad_up_low = (grad_up_act * gelu_grad(up_pre)).astype(bf16)
    grad_up_b = jnp.sum(grad_up_low.astype(f32), axis=0, keepdims=True)
    grad_up_w = contract(normed_low, grad_up_low, 0, 0).astype(bf16)
    grad_value_w = contract(normed_low, grad_value_low, 0, 1).astype(bf16)

    def own_and_theirs(x):
        x = x.reshape(T, 2, blocks, width)
        return lax.dynamic_index_in_dim(x, core, 1, False), lax.dynamic_index_in_dim(x, 1 - core, 1, False)

    def by_token(x):
        return x.transpose(1, 0, 2).reshape(tok, width)

    grad_part = contract(grad_up_low, up_w, 1, 1) + contract(grad_value_low, value_w, 0, 1)
    grad_gain = jnp.sum(grad_part * unit_chip, axis=0, keepdims=True)
    grad_shift = jnp.sum(grad_part, axis=0, keepdims=True)
    own_gf = own_g.astype(f32)
    grad_out_b = jnp.sum(own_gf, axis=(0, 1))[None]

    def split_parts(state):
        gated, part = state
        mine, theirs = zip(own_and_theirs(contract(gated, out_w, 1, 0)), own_and_theirs(part))
        return mine, jnp.stack([t.astype(bf16) for t in theirs])

    def exchange_parts(state):
        return state[0], swap(state[1])

    def finish_result(state):
        mine, came = state
        return by_token((own_x.astype(f32) + mine[0] + came[0] + wide[2]).astype(bf16)), mine[1] + came[1]

    def finish_tokens(state):
        result, grad_normed = state
        unit, scale = normalise(own_x)
        h = grad_normed * wide[0]
        inner = h - jnp.mean(h, axis=-1, keepdims=True) - unit * jnp.mean(h * unit, axis=-1, keepdims=True)
        return result, by_token(own_gf + inner * scale)

    if staged:
        vectors = (grad_skip, grad_value_b, grad_proj_b, grad_up_b, grad_gain, grad_shift, grad_out_b)
        small = small_sums(table, grad_mix, *vectors)
        grad_out_cross = swap(grad_out_send)
        work = [split_parts, exchange_parts, finish_result, finish_tokens, idle]
        grads = (grad_proj_mine, grad_proj_theirs, grad_out_mine, grad_out_cross, grad_up_w, grad_value_w, small)
        (mine, send), (result, grad_tokens) = scatter_all(*grads, work, (gated_low, grad_part))
        sum_proj_w, sum_out_w, sum_up_w, sum_value_w, sum_rate, sum_in, sum_out, *vectors = unpack(mine, swap(send))
        sum_step, sum_skip, sum_value_b, sum_proj_b, sum_up_b, sum_gain, sum_shift, sum_out_b = vectors
    else:

        grad_mix = grad_mix.T
        grad_weight, grad_decay = grad_mix[:, :64], grad_mix[:, 64:]
        product = out_p * in_p
        grad_ssm = (
            grad_decay * decay_log + grad_weight * (product * (decay * step - gap)),
            grad_weight * out_p * gap,
            grad_weight * in_p * gap,
            jnp.sum(grad_decay * decay_log + grad_weight * (product * decay * step), axis=1, keepdims=True),
        )

        def share(x):
            return lax.psum_scatter(x.astype(f32), both, scatter_dimension=0, tiled=True)

        def halves(x, axis):
            zero = jnp.zeros_like(x)
            return share(in_order(core, x, zero, axis))

        result, grad_tokens = finish_tokens(finish_result(exchange_parts(split_parts((gated_low, grad_part)))))
        sum_up_w, sum_value_w = halves(grad_up_w, 1), halves(grad_value_w, 1)
        sum_proj_w = halves(in_order(core, grad_proj_mine, grad_proj_theirs, 0), 1)
        sum_out_w = halves(in_order(core, grad_out_mine, grad_out_send, 1), 0)
        sum_rate, sum_in, sum_out, sum_step = (halves(v, 0) for v in grad_ssm)
        sum_step = sum_step[:, 0]
        sum_skip, sum_value_b, sum_proj_b = (halves(v, 0) for v in (grad_skip[:, 0], grad_value_b[:, 0], grad_proj_b[0]))
        sum_up_b = halves(grad_up_b[0], 0)
        sum_gain, sum_shift, sum_out_b = share(grad_gain[0]), share(grad_shift[0]), share(grad_out_b[0])

    return (
        result,
        grad_tokens,
        sum_up_w,
        sum_value_w,
        sum_proj_w,
        sum_out_w,
        sum_gain,
        sum_shift,
        sum_up_b,
        sum_value_b,
        sum_proj_b,
        sum_out_b,
        sum_rate,
        sum_step,
        sum_in,
        sum_out,
        sum_skip,
    )


def solution(mesh):
    rows, vector = P(("wide", "narrow"), None), P(("wide", "narrow"))
    sizes = dict(mesh.shape)
    return jax.shard_map(
        functools.partial(per_device, sizes),
        mesh=mesh,
        in_specs=(rows, vector, rows, rows, rows, rows, rows) + (vector,) * 6 + (rows, vector, rows, rows, vector),
        out_specs=(rows,) * 6 + (vector,) * 6 + (rows, vector, rows, rows, vector),
        check_vma=False,
    )
```

```python
import functools

import jax
import jax.numpy as jnp
from jax import lax
from jax.experimental import pallas as pl
from jax.experimental.pallas import tpu as pltpu
from jax.sharding import PartitionSpec as P

T = 32
NB = 32
f32, bf16 = jnp.float32, jnp.bfloat16

def iota(shape, dim): return lax.broadcasted_iota(jnp.int32, shape, dim)

def take(x, index, axis):
    return jnp.take_along_axis(x, index, axis=axis, mode="promise_in_bounds")

def turn(x, sign):
    row, lane = iota((8, 128), 0), iota((8, 128), 1)
    return take(x, (lane - sign * 32 * (row & 3)) & 127, 1)

def skew(x):
    row, chunk = iota((8, 128), 0), iota((8, 128), 1) >> 5
    return take(x, (row & 4) | ((chunk - row) & 3), 0)

def swap_chunks(x):
    return turn(skew(turn(x, 1)), -1)

def to_blocks(x):
    z = [swap_chunks(x[:, 128 * j:128 * j + 128]) for j in range(8)]
    low = iota((8, 128), 0) < 4
    left = [jnp.where(low, z[2 * i], pltpu.roll(z[2 * i + 1], 4, 0)) for i in range(4)]
    right = [jnp.where(low, pltpu.roll(z[2 * i], 4, 0), z[2 * i + 1]) for i in range(4)]
    return jnp.concatenate([jnp.concatenate(left, 0), jnp.concatenate(right, 0)], 1)

def from_blocks(y):
    low = iota((8, 128), 0) < 4
    out = []
    for i in range(4):
        l, r = y[8 * i:8 * i + 8, :128], y[8 * i:8 * i + 8, 128:]
        for z in (jnp.where(low, l, pltpu.roll(r, 4, 0)), jnp.where(low, pltpu.roll(l, 4, 0), r)):
            out.append(swap_chunks(z))
    return jnp.concatenate(out, 1)

def diagonal(y, half):
    part = y[:, 128 * half:128 * half + 128]
    chunk = iota(part.shape, 1) >> 5
    return jnp.concatenate([jnp.where(chunk == c, part, jnp.zeros_like(part)) for c in range(4)], 0)

def dot(a, b, dims=((1,), (0,))):
    return lax.dot_general(a, b, (dims, ((), ())), preferred_element_type=f32)

def two(parts): return jnp.concatenate(parts, 1)

def shift(x, k, back):
    n = 128 - k if back else k
    return two([pltpu.roll(x[:, :128], n, 1), pltpu.roll(x[:, 128:], n, 1)])

def spread(x3):
    r = ((iota((24, 256), 0) & 7) == (iota((24, 256), 1) >> 5)).astype(f32).astype(bf16)
    return dot(x3, r, ((0,), (0,)))

def roll_halves(x, amount, **kw):
    return two([pltpu.roll(x[:, :128], amount, 1, **kw), pltpu.roll(x[:, 128:], amount, 1, **kw)])

def lag_rows(row, amount):
    row = roll_halves(jnp.broadcast_to(row, (8, 256)), amount)
    return roll_halves(jnp.concatenate([row] * 4, 0), 0, stride=1, stride_axis=0)

def gelu_parts(x):
    k = 0.7978845608028654
    t = jnp.tanh(k * (x + 0.044715 * (x * x * x)))
    return t, k

def gelu(x):
    t, k = gelu_parts(x)
    return 0.5 * x * (1.0 + t)

def gelu_grad(x):
    t, k = gelu_parts(x)
    return 0.5 * (1.0 + t) + 0.5 * x * (1.0 - t * t) * k * (1.0 + 3 * 0.044715 * x * x)

def halved(x):
    hi = x.astype(bf16)
    return hi, (x - hi.astype(f32)).astype(bf16)

def each(f, *lists):
    return [f(*items) for items in zip(*lists)]

def scans(es, fs, mask_ref, first, back):
    for i in range(4):
        moved = each(lambda e: shift(e, 1 << i, back), es)
        m = mask_ref[first + i:first + i + 1, :]
        es = each(lambda e, f, s: e + (f * m) * s, es, fs, moved)
        if i < 3: fs = each(lambda f: f * f, fs)
    return es

def halves_dot(lhs, rights, width):
    return two([dot(lhs[:, width * h:width * h + width], rights[h]) for h in range(2)])

def fwd_groups(rev, xs, d3s, w3s, drows, wrows, skips, masks):
    vs = each(gelu, xs)
    vys = each(lambda v: to_blocks(v).astype(bf16), vs)
    d1s, w1s = each(spread, d3s), each(spread, w3s)
    pos = iota((64, 256), 1) & 31
    p = (pos if rev else 31 - pos).astype(f32)
    pts = each(lambda d1: jnp.exp(p * d1), d1s)
    krows = each(lambda w1, pt: jnp.sum(w1 * pt, axis=0, keepdims=True), w1s, pts)
    row, lane = iota((T, 256), 0), iota((T, 256), 1) & 31
    valid = (lane >= row if rev else row >= lane)
    toeps = each(lambda k: jnp.where(valid, lag_rows(k, 0 if rev else 97), 0.0), krows)
    lhss = each(lambda pt, t: jnp.concatenate([pt, t], 0).astype(bf16), pts, toeps)
    boths = each(lambda lhs, vy: halves_dot(lhs, [diagonal(vy, h) for h in range(2)], 128), lhss, vys)
    fs = each(lambda d1: jnp.exp(float(T) * d1), d1s)
    hs = scans([b[:64] for b in boths], fs, masks, 0, rev)
    hes = each(lambda h: masks[0:1, :] * shift(h, 1, rev), hs)
    col = iota((T, 512), 0)
    q = (T - col if rev else col + 1).astype(f32)
    leads = each(lambda wrow, drow: (wrow * jnp.exp(q * drow)).astype(bf16), wrows, drows)
    outers = each(lambda lead, he: halves_dot(lead, [diagonal(he.astype(bf16), h) for h in range(2)], 256), leads, hes)
    return each(lambda b, o, skip, v: from_blocks(b[64:] + o) + skip * v, boths, outers, skips, vs), hes

def fwd_kernel(groups, unroll, dir_ref, x_ref, d3_ref, w3_ref, drow_ref, wrow_ref, skip_ref, mask_ref, out_ref, enter_ref):
    def body(rev, i, _):
        gs = [i * unroll + u for u in range(unroll)]
        rows = [pl.ds(pl.multiple_of(g * 8, 8), 8) for g in gs]
        pick = lambda ref, at: [ref[a] for a in at]
        pickr = lambda ref: [ref[r, :] for r in rows]
        pickf = lambda ref: [ref[pl.ds(g, 1), :] for g in gs]
        outs, enters = fwd_groups(rev, pickr(x_ref), pick(d3_ref, gs), pick(w3_ref, gs), pickf(drow_ref), pickf(wrow_ref), pickr(skip_ref), mask_ref)
        for g, r, o, e in zip(gs, rows, outs, enters):
            out_ref[r, :] = o
            enter_ref[g] = e
        return 0
    for rev in (False, True):
        @pl.when(dir_ref[0] == int(rev))
        def _(rev=rev):
            lax.fori_loop(0, groups // unroll, functools.partial(body, rev), 0)

def flip_rows(y):
    row = iota((8, 128), 0)
    tiles = [[take(y[8 * i : 8 * i + 8, 128 * h : 128 * h + 128], 7 - row, 0) for h in range(2)] for i in (3, 2, 1, 0)]
    return jnp.concatenate([two(t) for t in tiles], 0)

def bwd_groups(rev, at_group, xs, gms, hes, d3s, w3s, drows, skips, masks):
    vs = each(gelu, xs)
    vys = each(lambda v: to_blocks(v).astype(bf16), vs)
    gfs = each(to_blocks, gms)
    gys = each(lambda g: g.astype(bf16), gfs)
    gyrs = each(lambda g: flip_rows(g).astype(bf16), gfs)
    d1s, w1s = each(spread, d3s), each(spread, w3s)
    pos = iota((64, 256), 1) & 31
    p = (pos if rev else 31 - pos).astype(f32)
    pts = each(lambda d1: jnp.exp(p * d1), d1s)
    ppts = each(lambda pt: p * pt, pts)
    rs = each(lambda d1: jnp.exp((31.0 - p) * d1), d1s)
    ats = each(lambda r, d1: r * jnp.exp(d1), rs, d1s)
    apts = each(lambda at: (32.0 - p) * at, ats)
    krows = each(lambda w1, r: jnp.sum(w1 * r, axis=0, keepdims=True), w1s, rs)
    row, lane = iota((T, 256), 0), iota((T, 256), 1) & 31
    ok2 = (row >= lane if rev else lane >= row)
    toeps = each(lambda k: jnp.where(ok2, lag_rows(k, 97 if rev else 0), 0.0), krows)
    lhs_v = each(lambda ppt: ppt.astype(bf16), ppts)
    lhs_g = each(lambda at, apt, t: jnp.concatenate([at, apt, t], 0).astype(bf16), ats, apts, toeps)
    bdvs = each(lambda vy: [diagonal(vy, h) for h in range(2)], vys)
    bdgs = each(lambda gy: [diagonal(gy, h) for h in range(2)], gys)
    ees = each(lambda l, b: halves_dot(l, b, 128), lhs_v, bdvs)
    qqs = each(lambda l, b: halves_dot(l, b, 128), lhs_g, bdgs)
    ms = each(lambda gy, b: two([dot(gy[:, 128 * h:128 * h + 128], b[h], ((1,), (1,))) for h in range(2)]), gyrs, bdvs)
    fs = each(lambda d1: jnp.exp(float(T) * d1), d1s)
    n = len(xs)
    downs = scans(each(lambda w1, q: w1 * q[:64], w1s, qqs), fs, masks, 4, not rev)
    des = each(lambda h: masks[4:5, :] * shift(h, 1, not rev), downs)
    col = iota((T, 512), 0)
    pw = (col if rev else 31 - col).astype(f32)
    p2s = each(lambda drow: jnp.exp(pw * drow).astype(bf16), drows)
    dvs = each(lambda qq, p2, de: qq[128:] + halves_dot(p2, [diagonal(de.astype(bf16), h) for h in range(2)], 256), qqs, p2s, des)
    ok = (lane + row >= 31 if rev else lane + row <= 31)
    ms = each(lambda m: roll_halves(jnp.where(ok, m, 0.0), 0, stride=1, stride_axis=0), ms)
    dks = each(lambda m: jnp.sum(m, axis=0, keepdims=True), ms)
    if rev: dks = each(lambda dk: roll_halves(jnp.broadcast_to(dk, (8, 256)), 97)[:1], dks)
    zws = each(lambda he, qq, pt, dk: he * qq[:64] + pt * dk, hes, qqs, pts, dks)
    zds = each(lambda w1, he, qq, ppt, dk, de, ee, f: w1 * (he * qq[64:128] + ppt * dk) + de * (ee + float(T) * f * he), w1s, hes, qqs, ppts, dks, des, ees, fs)
    total = 0.0
    for u, (zw, zd) in enumerate(zip(zws, zds)):
        column = 8 * (at_group + u) + (iota((256, 128), 0) >> 5)
        ones = (iota((256, 128), 1) == column).astype(f32).astype(bf16)
        both = dot(jnp.concatenate([*halved(zw), *halved(zd)], 0), ones)
        total = total + jnp.concatenate([both[:64] + both[64:128], both[128:192] + both[192:]], 0)
    dvals = each(lambda dv, skip, gm, x: (from_blocks(dv) + skip * gm) * gelu_grad(x), dvs, skips, gms, xs)
    dskips = each(lambda gm, v: jnp.sum(gm * v, axis=1, keepdims=True), gms, vs)
    return dvals, total, dskips

def bwd_kernel(groups, unroll, dir_ref, x_ref, gm_ref, enter_ref, d3_ref, w3_ref, drow_ref, skip_ref, mask_ref, gv_ref, grads_ref, dskip_ref, dbias_ref):
    grads_ref[...] = jnp.zeros_like(grads_ref)
    def body(rev, i, _):
        gs = [i * unroll + u for u in range(unroll)]
        rows = [pl.ds(pl.multiple_of(g * 8, 8), 8) for g in gs]
        pick = lambda ref: [ref[a] for a in gs]
        pickr = lambda ref: [ref[r, :] for r in rows]
        pickf = lambda ref: [ref[pl.ds(g, 1), :] for g in gs]
        gms = pickr(gm_ref)
        dvals, total, dskips = bwd_groups(rev, i * unroll, pickr(x_ref), gms, pick(enter_ref), pick(d3_ref), pick(w3_ref), pickf(drow_ref), pickr(skip_ref), mask_ref)
        grads_ref[...] += total
        for r, a, c in zip(rows, dvals, dskips):
            dskip_ref[r, :] = c
            dbias_ref[r, :] = jnp.sum(a.astype(bf16).astype(f32), axis=1, keepdims=True)
        for u in range(0, unroll, 2):
            gv_ref[pl.ds(pl.multiple_of((i * unroll + u) * 8, 16), 16), :] = jnp.concatenate(dvals[u : u + 2], 0).astype(bf16)
        return 0
    for rev in (False, True):
        @pl.when(dir_ref[0] == int(rev))
        def _(rev=rev):
            lax.fori_loop(0, groups // unroll, functools.partial(body, rev), 0)

def specs(cb, first):
    g = cb // 8
    rows = lambda lanes: pl.BlockSpec((cb, lanes), lambda i: (i + first, 0))
    per = lambda a, b: pl.BlockSpec((g, a, b), lambda i: (i + first, 0, 0))
    flat = lambda lanes: pl.BlockSpec((g, lanes), lambda i: (i + first, 0))
    return rows, per, flat

def mix_call(kernel, name, out_shape, in_specs, out_specs, steps, done, args):
    n = len(args)
    if done is None:
        body, aliases, done = kernel, {}, ()
    else:
        body = lambda *refs: kernel(*refs[:n], *refs[n + len(done):])
        aliases = {n + i: i for i in range(len(done))}
        in_specs = in_specs + [pl.BlockSpec(memory_space=pl.ANY)] * len(done)
    return pl.pallas_call(
        body,
        out_shape=out_shape,
        grid=(steps,),
        in_specs=in_specs,
        out_specs=out_specs,
        input_output_aliases=aliases,
        compiler_params=pltpu.CompilerParams(vmem_limit_bytes=60 << 20),
        name=name,
    )(*args, *done)

MASKS = pl.BlockSpec((8, 256), lambda i: (0, 0))
SCALAR = pl.BlockSpec(memory_space=pltpu.SMEM)

def ssm_fwd(direction, x, d3, w3, drow, wrow, skip, masks, part=0, parts=1, done=None, cb=64, unroll=8):
    c, tok = x.shape
    steps = c // cb // parts
    rows, per, flat = specs(cb, part * steps)
    return mix_call(
        functools.partial(fwd_kernel, cb // 8, unroll),
        f"mix_forward_{part}",
        (jax.ShapeDtypeStruct((c, tok), f32), jax.ShapeDtypeStruct((c // 8, 64, 256), f32)),
        [SCALAR, rows(tok), per(24, 64), per(24, 64), flat(512), flat(512), rows(1), MASKS],
        (rows(tok), per(64, 256)),
        steps, done, (direction, x, d3, w3, drow, wrow, skip, masks),
    )

def ssm_bwd(direction, x, gm, enter, d3, w3, drow, skip, masks, part=0, parts=1, done=None, cb=128, unroll=8):
    c, tok = x.shape
    steps = c // cb // parts
    first = part * steps
    rows, per, flat = specs(cb, first)
    return mix_call(
        functools.partial(bwd_kernel, cb // 8, unroll),
        f"mix_backward_{part}",
        (jax.ShapeDtypeStruct((c, tok), bf16), jax.ShapeDtypeStruct((128, c), f32), jax.ShapeDtypeStruct((c, 1), f32), jax.ShapeDtypeStruct((c, 1), f32)),
        [SCALAR, rows(tok), rows(tok), per(64, 256), per(24, 64), per(24, 64), flat(512), rows(1), MASKS],
        (rows(tok), pl.BlockSpec((128, cb), lambda i: (0, i + first)), rows(1), rows(1)),
        steps, done, (direction, x, gm, enter, d3, w3, drow, skip, masks),
    )

def thirds(x):
    hi = x.astype(bf16)
    rest = x - hi.astype(f32)
    mid = rest.astype(bf16)
    lo = (rest - mid.astype(f32)).astype(bf16)
    c = x.shape[0]
    return jnp.concatenate([a.reshape(c // 8, 8, 64) for a in (hi, mid, lo)], 1)

def block_masks(labels, rev):
    idx = jnp.arange(16)[None, :]
    def reach(k, back):
        other = jnp.roll(labels, -k if back else k, axis=1)
        inside = (idx + k < 16) if back else (idx >= k)
        return (inside & (other == labels)).astype(f32).reshape(32)
    ahead = jnp.stack([reach(k, False) for k in (1, 2, 4, 8)])
    behind = jnp.stack([reach(k, True) for k in (1, 2, 4, 8)])
    both = jnp.where(rev, jnp.concatenate([behind, ahead]), jnp.concatenate([ahead, behind]))
    return jnp.tile(both, (1, 8))


ROUNDS = (
    {"x": "own", "y": "own", "z": "own", "o": "own", "m": "own"},
    {"x": (0, "y"), "y": (0, "z"), "z": (0, "m"), "o": (0, "x"), "m": (0, "z")},
    {"x": (1, "y"), "y": (1, "z"), "z": (1, "m"), "o": (1, "z"), "m": (1, "y")},
    {"x": (2, "z"), "y": (2, "z"), "z": (0, "x"), "o": (0, "x"), "m": (2, "x")},
    {"x": (2, "y"), "y": (3, "x"), "z": (3, "x"), "o": (3, "x")},
)
PERMS = {
    "x": [(w, w ^ 1) for w in range(16)],
    "y": [(w, w ^ 2) for w in range(16)],
    "z": [(w, w ^ 4) for w in range(16)],
    "m": [(w, w + 4) for w in range(4, 8)] + [(w, w - 4) for w in range(8, 12)],
}


def trace_rounds():
    end, mid = {"own": (0, 0, 0)}, {"own": (0, 0, 1)}
    for r, sends in enumerate(ROUNDS):
        new_end, new_mid = {}, {}
        for d, bit in (("x", 0), ("y", 1)):
            for held, new in ((end, new_end), (mid, new_mid)):
                item = list(held[sends[d]])
                item[bit] ^= 1
                new[(r, d)] = tuple(item)
        new_end[(r, "z")], new_mid[(r, "z")] = mid[sends["z"]], end[sends["o"]]
        if "m" in sends:
            dx, dy, layer = mid[sends["m"]]
            new_end[(r, "m")], new_mid[(r, "m")] = None, (dx, dy, 3 - layer)
        end.update(new_end)
        mid.update(new_mid)

    def firsts(held):
        seen, first = set(), {}
        for slot, item in held.items():
            first[slot] = item is not None and item not in seen
            seen.add(item)
        return first

    return end, mid, firsts(end), firsts(mid)


END, MID, FIRST_END, FIRST_MID = trace_rounds()
SLOTS = tuple(END)


def at_end():
    layer = lax.axis_index("wide") >> 2
    return (layer == 0) | (layer == 3)


def owner(slot):
    w = lax.axis_index("wide")
    x, y, layer = w & 1, (w >> 1) & 1, w >> 2

    def of(held):
        dx, dy, z = held[slot] or (0, 0, 0)
        return jnp.where(layer >= 2, 3 - z, z) * 4 + (y ^ dy) * 2 + (x ^ dx)

    return jnp.where(at_end(), of(END), of(MID))


def is_first(slot):
    return jnp.where(at_end(), int(FIRST_END[slot]), int(FIRST_MID[slot]))


def core_index():
    return lax.axis_index("narrow") & 1


def within_half(w, rows):
    return pl.multiple_of((w & 7) * rows, 16)


ANY = pl.BlockSpec(memory_space=pl.ANY)
HBM = pl.BlockSpec(memory_space=pltpu.HBM)
VM = pl.BlockSpec(memory_space=pltpu.VMEM)


def params(mib=60):
    return pltpu.CompilerParams(vmem_limit_bytes=mib << 20)


def shape(dims, dtype):
    return jax.ShapeDtypeStruct(dims, dtype)


def ones_where(condition):
    return jnp.where(condition, 1.0, 0.0).astype(bf16)


def pack_kernel(up, value, proj, out, rate, in_map, out_map, *refs):
    *vectors, keep, send, rows = refs
    def lanes(n, first):
        return ones_where(iota((n, 256), 1) == iota((n, 256), 0) + first)

    rows[...] = jnp.zeros((16, 48), f32)
    k = 0
    for ref in vectors:
        v = ref[...].astype(f32)
        for first in range(0, v.shape[0], 48):
            part = v[first : first + 48]
            rows[k, : part.shape[0]] = part
            k += 1
    small = dot(rows[...].astype(bf16), lanes(16, 192), ((0,), (0,)))
    for k, ref in enumerate((rate, in_map, out_map)):
        small = small + dot(ref[...], lanes(64, 64 * k))
    for core in range(2):

        @pl.when(core_index() == core)
        def _(core=core):
            for ref, half in ((keep, core), (send, 1 - core)):
                a = up[...].astype(f32)
                for q in range(2):
                    ref[24 * q : 24 * q + 24, :] = a[:, 1536 * half + 768 * q : 1536 * half + 768 * q + 768]
                ref[48:72, :] = value[...].astype(f32)[:, 768 * half : 768 * half + 768]
                ref[72:168, :] = proj[...].astype(f32)[:, 768 * half : 768 * half + 768]
                b = out[...].astype(f32)[:, 384 * half : 384 * half + 384]
                ref[168:192, :384] = b[:24]
                ref[168:192, 384:] = b[24:]
                for j in range(3):
                    ref[192:208, 256 * j : 256 * j + 256] = small[16 * j : 16 * j + 16, :]


def pack(*shards):
    return pl.pallas_call(
        pack_kernel,
        out_shape=(shape((208, 768), f32),) * 2,
        in_specs=[VM] * len(shards),
        out_specs=(VM, VM),
        scratch_shapes=[pltpu.VMEM((16, 48), f32)],
        compiler_params=params(),
        name="pack_shards",
    )(*shards)


def merge_kernel(keep, recv, blob):
    for core in range(2):

        @pl.when(core_index() == core)
        def _(core=core):
            lo, hi = (keep, recv) if core == 0 else (recv, keep)

            def both(a, n):
                return jnp.concatenate([lo[a : a + n, :], hi[a : a + n, :]], 0)

            for q in range(2):
                blob[48 * q : 48 * q + 48, :] = both(24 * q, 24).astype(bf16)
            blob[96:144, :] = both(48, 24).astype(bf16)
            s = [ref[192:208, 256 * j : 256 * j + 256] for ref in (lo, hi) for j in range(3)]
            for j in range(3):
                blob[144:176, 256 * j : 256 * j + 256] = jnp.concatenate(s[2 * j : 2 * j + 2], 0).astype(bf16)
            blob[176:368, :] = both(72, 96).astype(bf16)
            for k, ref in enumerate((lo, hi)):
                rows = jnp.concatenate([ref[168:192, :384], ref[168:192, 384:]], 0)
                blob[368:416, 384 * k : 384 * k + 384] = rows.astype(bf16)


def merge(keep, recv):
    return pl.pallas_call(
        merge_kernel,
        out_shape=shape((416, 768), bf16),
        in_specs=[VM, VM],
        out_specs=VM,
        compiler_params=params(),
        name="merge_pair",
    )(keep, recv)


def together(*trees):
    return lax.optimization_barrier(trees)


def gather_rounds(own, work, state=None):
    held = {"own": own}
    end = at_end()
    for r, sends in enumerate(ROUNDS):
        blocks = {}
        for d in "xyzm":
            if d in sends:
                block = held[sends[d]]
                if d == "z" and sends["z"] != sends["o"]:
                    block = jnp.where(end, held[sends["o"]], block)
                blocks[d] = block
        blocks, state = together(blocks, state)
        came = {d: lax.ppermute(block, "wide", PERMS[d]) for d, block in blocks.items()}
        state = work[r](state)
        if r == len(ROUNDS) - 1:
            early = dict(held)
            early[sends["x"]] = blocks["x"]
            placed = place_all(tuple(early), tuple(early.values()))
            came, placed, state = together(came, placed, state)
            late = {(r, d): block for d, block in came.items()}
            return place_all(tuple(late), tuple(late.values()), placed), state
        came, state = together(came, state)
        held.update({(r, d): block for d, block in came.items()})


def place_kernel(slots, pieces, outs, held, *refs):
    n = len(slots)
    blocks, refs = refs[:n], refs[n + held :]
    dests, (buf, in_sem, out_sem) = refs[:outs], refs[outs:]

    def each_slot(act):
        for i, slot in enumerate(slots):
            if FIRST_END[slot] and FIRST_MID[slot]:
                act(i, owner(slot))
            else:
                pl.when(is_first(slot) == 1)(functools.partial(act, i, owner(slot)))

    def load(i):
        return pltpu.make_async_copy(blocks[i], buf.at[i], in_sem.at[i])

    def stores(i, w):
        mine = (w >> 3) == core_index()
        for src, which, dst in pieces:

            def go(at, src=src, dst=dst):
                pltpu.make_async_copy(buf.at[(i,) + src], dests[at].at[dst(w)], out_sem.at[i]).start()

            if isinstance(which, int):
                go(which)
            else:
                pl.when(mine)(functools.partial(go, which[0]))
                pl.when(jnp.logical_not(mine))(functools.partial(go, which[1]))

    def load_start(i, w):
        load(i).start()

    def pass_on(i, w):
        load(i).wait()
        stores(i, w)

    def finish(i, w):
        pltpu.make_async_copy(blocks[i], buf.at[i], out_sem.at[i]).wait()

    for act in (load_start, pass_on, finish):
        each_slot(act)


def place(slots, blocks, pieces, out_shapes, done, name):
    n, held = len(slots), len(done)
    return pl.pallas_call(
        functools.partial(place_kernel, slots, pieces, len(out_shapes), held),
        out_shape=out_shapes,
        in_specs=[ANY] * (n + held),
        out_specs=tuple(ANY for _ in out_shapes),
        input_output_aliases={n + k: k for k in range(held)},
        scratch_shapes=[
            pltpu.VMEM((n,) + blocks[0].shape, bf16),
            pltpu.SemaphoreType.DMA((n,)),
            pltpu.SemaphoreType.DMA((n,)),
        ],
        compiler_params=params(),
        name=name,
    )(*blocks, *done)


def place_all(slots, blocks, done=()):
    full = slice(None)
    pieces = [
        ((slice(0, 48), full), 0, lambda w: (pl.ds(pl.multiple_of(w * 48, 16), 48), slice(0, 768))),
        ((slice(48, 96), full), 0, lambda w: (pl.ds(pl.multiple_of(w * 48, 16), 48), slice(768, 1536))),
        ((slice(96, 144), full), 1, lambda w: (pl.ds(pl.multiple_of(w * 48, 16), 48), full)),
        ((slice(176, 368), full), (3, 4), lambda w: (pl.ds(within_half(w, 192), 192), full)),
    ]
    for j in range(3):
        pieces.append(
            (
                (slice(144, 176), slice(256 * j, 256 * j + 256)),
                2,
                lambda w, j=j: (pl.ds(pl.multiple_of(w * 96 + 32 * j, 16), 32), full),
            )
        )
    for k in range(2):
        pieces.append(
            (
                (slice(368, 416), slice(384 * k, 384 * k + 384)),
                (5, 6),
                lambda w, k=k: (pl.ds(within_half(w, 96) + 48 * k, 48), full),
            )
        )
    dims = ((768, 1536), (768, 768), (1536, 256), (1536, 768), (1536, 768), (768, 384), (768, 384))
    name = "place_last" if done else "place_first"
    return place(slots, blocks, pieces, tuple(shape(d, bf16) for d in dims), done, name)


def divided_by_48(x):
    return (x * 1366) >> 16


def row_of_wide(shape_of, width_dim):
    d = iota(shape_of, width_dim)
    w = divided_by_48(d)
    rest = d - 48 * w
    c = jnp.where(rest >= 24, 1, 0)
    return 96 * w + 48 * c + rest - 24 * c


def row_of_up(shape_of, up_dim):
    f = iota(shape_of, up_dim)
    q = divided_by_48(f)
    return 96 * (q >> 2) + 48 * ((q >> 1) & 1) + f - 48 * q, q & 1


def mix_parameters(mine):
    rate = -jnp.exp(mine[:, :64])
    step = jnp.exp(mine[:, 192:193])
    decay_log = step * rate
    decay = jnp.exp(decay_log)
    gap = (decay - 1.0) / rate
    return rate, step, decay_log, decay, gap


def coefficients_kernel(table, labels, d3, w3, drow, wrow, skip, value_b, proj_b, up_b, wide, masks, buf):
    half = pl.ds(pl.multiple_of(core_index() * 768, 256), 768)
    mine = table[half, :].astype(f32)
    rate, step, decay_log, decay, gap = mix_parameters(mine)
    weight = mine[:, 128:192] * gap * mine[:, 64:128]
    for v, three, row in ((decay_log, d3, drow), (weight, w3, wrow)):
        parts, rest = [], v
        for _ in range(3):
            part = rest.astype(bf16).astype(f32)
            parts.append(part.reshape(96, 8, 64))
            rest = rest - part
        three[...] = jnp.concatenate(parts, 1).astype(bf16)
        buf[...] = v
        for c in range(8):
            row[:, 64 * c : 64 * c + 64] = buf[pl.ds(c, 96, stride=8), :]
    skip[...] = mine[:, 193:194]
    value_b[...] = mine[:, 194:195]
    low = table[half, 128:]
    proj_b[...] = mine[:, 128:].T[67:68, :]
    r, k = row_of_up((768, 1536), 1)
    at = r == iota((768, 1536), 0)
    pick = lambda which: dot(low, ones_where(at & (k == which)), ((0,), (0,)))
    up_b[...] = pick(0)[68:69, :] + pick(1)[69:70, :]
    spread_wide = ones_where(row_of_wide((1536, 768), 1) == iota((1536, 768), 0))
    wide[...] = dot(table[:, 128:], spread_wide, ((0,), (0,)))[70:73, :]
    lane = iota((8, 256), 1)
    each_lane = ones_where((iota((32, 256), 1) & 31) == iota((32, 256), 0))
    label = dot(jnp.broadcast_to(labels[...], (8, 32)).astype(bf16), each_lane)
    rows = []
    for k in (1, 2, 4, 8):
        before = jnp.where(((lane & 15) >= k) & (roll_halves(label, k) == label), 1.0, 0.0)
        behind = jnp.where(((lane & 15) + k < 16) & (roll_halves(label, 128 - k) == label), 1.0, 0.0)
        rows.append((before, behind))
    back = core_index() == 1
    for i, (before, behind) in enumerate(rows):
        masks[i : i + 1, :] = jnp.where(back, behind, before)[:1]
        masks[4 + i : 5 + i, :] = jnp.where(back, before, behind)[:1]


def coefficients(table, labels):
    dims = [((96, 24, 64), bf16)] * 2 + [((96, 512), f32)] * 2 + [((768, 1), f32)] * 2 + [((1, 768), f32), ((1, 1536), f32), ((3, 768), f32), ((8, 256), f32)]
    return pl.pallas_call(
        coefficients_kernel,
        out_shape=tuple(shape(*d) for d in dims),
        in_specs=[VM, VM],
        out_specs=(VM,) * len(dims),
        scratch_shapes=[pltpu.VMEM((768, 64), f32)],
        compiler_params=params(),
        name="coefficients",
    )(table, labels)


def small_sums_kernel(table, grads, skip, value_b, proj_b, up_b, gain, shift, out_b, out, buf, turn_buf):
    half = pl.ds(pl.multiple_of(core_index() * 768, 256), 768)
    theirs = pl.ds(pl.multiple_of((1 - core_index()) * 768, 256), 768)
    mine = table[half, :].astype(f32)
    rate, step, decay_log, decay, gap = mix_parameters(mine)
    in_p, out_p = mine[:, 64:128], mine[:, 128:192]
    both = grads[...].T
    weight, slope = both[:, :64], both[:, 64:]
    product = out_p * in_p
    through = slope * decay_log
    buf[theirs, :] = jnp.zeros((768, 256), f32)
    buf[half, 128:] = jnp.zeros((768, 128), f32)
    turn_buf[...] = jnp.zeros((128, 128), f32)
    buf[half, 0:64] = through + weight * (product * (decay * step - gap))
    buf[half, 64:128] = weight * out_p * gap
    buf[half, 128:192] = weight * in_p * gap
    buf[half, 192:193] = jnp.sum(through + weight * (product * decay * step), axis=1, keepdims=True)
    for k, ref in enumerate((skip, value_b)):
        buf[half, 193 + k : 194 + k] = ref[...]
    buf[half, 195:196] = jnp.broadcast_to(proj_b[...], (8, 768)).T[:, :1]
    units, widths = up_b[...], [ref[...] for ref in (gain, shift, out_b)]
    for q in range(32):
        turn_buf[q, 0:48] = units[48 * q : 48 * q + 48]
        for k, v in enumerate(widths):
            turn_buf[32 + 3 * q + k, 0:24] = v[24 * q : 24 * q + 24]
    columns = turn_buf[...].T
    for q in range(16):
        buf[pl.ds(pl.multiple_of(core_index() * 768 + 48 * q, 16), 48), 196:198] = columns[:48, 2 * q : 2 * q + 2]
    for q in range(32):
        buf[48 * q : 48 * q + 24, 198:201] = columns[:24, 32 + 3 * q : 35 + 3 * q]
    for w in range(16):
        for j in range(3):
            out[w, :, 256 * j : 256 * j + 256] = buf[96 * w + 32 * j : 96 * w + 32 * j + 32, :]


def small_sums(*args):
    return pl.pallas_call(
        small_sums_kernel,
        out_shape=shape((16, 32, 768), f32),
        in_specs=[VM] * len(args),
        out_specs=VM,
        scratch_shapes=[pltpu.VMEM((1536, 256), f32), pltpu.VMEM((128, 128), f32)],
        compiler_params=params(),
        name="small_sums",
    )(*args)


def children_of():
    kids = {s: [] for s in SLOTS}
    for r, sends in enumerate(ROUNDS):
        for d in "xyzm":
            if d not in sends:
                continue
            if d != "z" or sends["z"] == sends["o"]:
                kids[sends[d]].append(((r, d), None))
            else:
                kids[sends["z"]].append(((r, "z"), "mid"))
                kids[sends["o"]].append(((r, "z"), "end"))
    return kids


KIDS = children_of()


def sum_kernel(slots, pieces, n_own, arrived, rows, final, *refs):
    owns, refs = refs[:n_own], refs[n_own:]
    ins, refs = refs[: len(arrived)], refs[len(arrived) :]
    n_out = 2 if final else len(slots)
    outs, (own_buf, small_buf, in_buf, out_buf, own_sem, small_sem, in_sem, out_sem) = refs[:n_out], refs[n_out:]
    in_copies = []

    def start_own(p):
        w = owner(slots[p])
        mine = (w >> 3) == core_index()
        for choices, dst in pieces:
            for choice, (which, src) in enumerate(choices):

                def go(which=which, src=src, dst=dst):
                    buf, sem = (own_buf, own_sem) if owns[which].dtype == bf16 else (small_buf, small_sem)
                    pltpu.make_async_copy(owns[which].at[src(w)], buf.at[(p,) + dst], sem.at[p]).start()

                if len(choices) == 1:
                    go()
                else:
                    pl.when(mine == (choice == 0))(go)

    def wait_own(p):
        for buf, sem in ((own_buf, own_sem), (small_buf, small_sem)):
            pltpu.make_async_copy(buf.at[p], buf.at[p], sem.at[p]).wait()

    for p in range(len(slots)):
        start_own(p)
    for k in range(len(arrived)):
        in_copies.append(pltpu.make_async_copy(ins[k], in_buf.at[k], in_sem.at[k]))
        in_copies[-1].start()
    end = at_end()
    waited = set()
    sent = []
    for p, slot in enumerate(slots):
        wait_own(p)
        parts = []
        for kid, layers in KIDS[slot]:
            k = arrived.index(kid)
            if k not in waited:
                in_copies[k].wait()
                waited.add(k)
            parts.append((k, None if layers is None else jnp.where(end == (layers == "end"), 1.0, 0.0)))
        whole = FIRST_END[slot] and FIRST_MID[slot]
        keep = None if whole else is_first(slot).astype(f32)

        def add(i, _, p=p, parts=parts, keep=keep, own=own_buf, first=0):
            at = pl.ds(pl.multiple_of(i * 32, 32), 32)
            to = pl.ds(pl.multiple_of(first + i * 32, 32), 32)
            total = own[p, at, :].astype(f32)
            if keep is not None:
                total = total * keep
            for k, mask in parts:
                v = in_buf[k, to, :].astype(f32)
                total = total + (v if mask is None else v * mask)
            out_buf[p, to, :] = total.astype(out_buf.dtype)
            return 0

        low_rows, small_rows = own_buf.shape[1], small_buf.shape[1]
        lax.fori_loop(0, low_rows // 32, add, 0, unroll=4)
        lax.fori_loop(0, small_rows // 32, functools.partial(add, own=small_buf, first=low_rows), 0)
        if not final:
            sent.append(pltpu.make_async_copy(out_buf.at[p], outs[p], out_sem.at[p]))
            sent[-1].start()
    if final:
        for i, (ref, core) in enumerate(((outs[0], core_index()), (outs[1], 1 - core_index()))):
            for k, (src, dst) in enumerate(final):
                sent.append(pltpu.make_async_copy(out_buf.at[(0,) + src(core)], ref.at[dst], out_sem.at[i * len(final) + k]))
                sent[-1].start()
    for c in sent:
        c.wait()


def sum_slots(slots, owns, pieces, came, rows, final=None, final_rows=None, name="sum"):
    arrived = []
    for slot in slots:
        for kid, _ in KIDS[slot]:
            if kid not in arrived:
                arrived.append(kid)
    if final:
        out_shapes = (shape((final_rows, 768), f32),) * 2
    else:
        out_shapes = tuple(shape((rows, 768), bf16) for _ in slots)
    return pl.pallas_call(
        functools.partial(sum_kernel, slots, pieces, len(owns), arrived, rows, final),
        out_shape=out_shapes,
        in_specs=[ANY] * (len(owns) + len(arrived)),
        out_specs=tuple(HBM for _ in out_shapes),
        scratch_shapes=[
            pltpu.VMEM((len(slots), rows - 32, 768), bf16),
            pltpu.VMEM((len(slots), 32, 768), f32),
            pltpu.VMEM((max(1, len(arrived)), rows, 768), bf16),
            pltpu.VMEM((len(slots), rows, 768), f32 if final else bf16),
            pltpu.SemaphoreType.DMA((len(slots),)),
            pltpu.SemaphoreType.DMA((len(slots),)),
            pltpu.SemaphoreType.DMA((max(1, len(arrived)),)),
            pltpu.SemaphoreType.DMA((2 * len(final) if final else len(slots),)),
        ],
        compiler_params=params(),
        name=name,
    )(*owns, *[came[k] for k in arrived])


def scatter_rounds(owns, pieces, rows, final, final_rows, name, work, state=None):
    came = {}
    for r in reversed(range(len(ROUNDS))):
        slots = [(r, d) for d in "xyzm" if d in ROUNDS[r]]
        blocks = sum_slots(slots, owns, pieces, came, rows, name=f"{name}_{r}")
        blocks, state = together(blocks, state)
        new = {slot: lax.ppermute(block, "wide", PERMS[slot[1]]) for slot, block in zip(slots, blocks)}
        state = work[len(ROUNDS) - 1 - r](state)
        new, state = together(new, state)
        came.update(new)
    return sum_slots(["own"], owns, pieces, came, rows, final, final_rows, name=f"{name}_own"), state


def scatter_all(proj_mine, proj_theirs, out, out_theirs, up, value, small, work, state):
    full = slice(None)

    pieces = [([(i, lambda w: (pl.ds(within_half(w, 192), 192), full)) for i in (0, 1)], (slice(0, 192), full))]
    for k in range(2):
        pieces.append(
            (
                [(i, lambda w, k=k: (pl.ds(within_half(w, 96) + 48 * k, 48), full)) for i in (2, 3)],
                (slice(192, 240), slice(384 * k, 384 * k + 384)),
            )
        )
        pieces.append(
            (
                [(4, lambda w, k=k: (pl.ds(pl.multiple_of(w * 48, 16), 48), slice(768 * k, 768 * k + 768)))],
                (slice(240 + 48 * k, 288 + 48 * k), full),
            )
        )
    pieces.append(([(5, lambda w: (pl.ds(pl.multiple_of(w * 48, 16), 48), full))], (slice(336, 384), full)))
    pieces.append(([(6, lambda w: (w,))], (slice(0, 32), full)))
    final = [
        (lambda c: (pl.ds(pl.multiple_of(c * 96, 8), 96), full), (slice(0, 96), full)),
        (lambda c: (slice(192, 240), pl.ds(pl.multiple_of(c * 384, 128), 384)), (slice(96, 144), slice(0, 384))),
        (lambda c: (slice(384, 416), full), (slice(216, 248), full)),
    ] + [
        (
            lambda c, q=q: (pl.ds(pl.multiple_of(240 + q * 48 + c * 24, 8), 24), full),
            (slice(144 + 24 * q, 168 + 24 * q), full),
        )
        for q in range(3)
    ]
    owns = (proj_mine, proj_theirs, out, out_theirs, up, value, small)
    return scatter_rounds(owns, pieces, 416, final, 248, "sum", work, state)


def unpack_kernel(mine, recv, proj, out, up, value, rate, in_map, out_map, *refs):
    *vectors, small = refs
    for core in range(2):

        @pl.when(core_index() == core)
        def _(core=core):
            for ref, half in ((mine, core), (recv, 1 - core)):
                proj[:, 768 * half : 768 * half + 768] = ref[:96, :]
                out[:, 384 * half : 384 * half + 384] = ref[96:144, :384]
                for q in range(2):
                    up[:, 1536 * half + 768 * q : 1536 * half + 768 * q + 768] = ref[144 + 24 * q : 168 + 24 * q, :]
                value[:, 768 * half : 768 * half + 768] = ref[192:216, :]
            s = mine[216:248, :] + recv[216:248, :]
            if core == 0:
                small[:32, :] = s[:, :256]
                small[32:, :] = s[:16, 256:512]
            else:
                small[:16, :] = s[16:, 256:512]
                small[16:, :] = s[:, 512:]

    rate[...] = small[:, :64]
    in_map[...] = small[:, 64:128]
    out_map[...] = small[:, 128:192]
    rows = small[:, 128:].T
    for k, ref in enumerate(vectors[:4] + vectors[5:]):
        row = 64 + k if k < 4 else 66 + k
        ref[...] = rows[row, : ref.shape[0]]
    vectors[4][0:48] = rows[68, :]
    vectors[4][48:96] = rows[69, :]


def unpack(mine, recv):
    dims = ((96, 1536), (48, 768), (24, 3072), (24, 1536), (48, 64), (48, 64), (48, 64)) + ((48,),) * 4 + ((96,), (24,), (24,), (24,))
    return pl.pallas_call(
        unpack_kernel,
        out_shape=tuple(shape(d, f32) for d in dims),
        in_specs=[VM, VM],
        out_specs=(VM,) * len(dims),
        scratch_shapes=[pltpu.VMEM((48, 256), f32)],
        compiler_params=params(),
        name="unpack_sums",
    )(mine, recv)


TILE = 256


def tokens_by(width):
    return pl.BlockSpec((TILE, width), lambda i: (i, 0))


def by_tokens(rows):
    return pl.BlockSpec((rows, TILE), lambda i: (0, i))


def whole_block(*dims):
    return pl.BlockSpec(dims, lambda i: (0,) * len(dims))


def enter_kernel(unit, wide, up_w, up_b, value_w, value_b, normed, up_pre, up_low, value_pre):
    low = (unit[...] * wide[0:1, :] + wide[1:2, :]).astype(bf16)
    normed[...] = low
    value_pre[...] = dot(low, value_w[...]).T + value_b[...]
    for k in range(0, up_w.shape[1], 512):
        at = slice(k, k + 512)
        pre = dot(low, up_w[:, at]) + up_b[:, at]
        up_pre[:, at] = pre
        up_low[:, at] = gelu(pre).astype(bf16)


def enter(unit, wide, up_w, up_b, value_w, value_b):
    n, d = unit.shape
    f, c = up_w.shape[1], value_w.shape[1]
    return pl.pallas_call(
        enter_kernel,
        out_shape=(shape((n, d), bf16), shape((n, f), f32), shape((n, f), bf16), shape((c, n), f32)),
        grid=(n // TILE,),
        in_specs=[tokens_by(d)] + [whole_block(*v.shape) for v in (wide, up_w, up_b, value_w, value_b)],
        out_specs=(tokens_by(d), tokens_by(f), tokens_by(f), by_tokens(c)),
        compiler_params=params(),
        name="enter",
    )(unit, wide, up_w, up_b, value_w, value_b)


def gate_kernel(up, up_other, g, mixed, proj_mine, proj_theirs, proj_b, out_a, out_b, gm, gated, gp, grad_b, grad_mine, grad_theirs, grad_out, grad_send, acc, acc_out, out_w):
    step, steps = pl.program_id(0), pl.num_programs(0)

    @pl.when(step == 0)
    def _():
        acc[...] = jnp.zeros_like(acc)
        acc_out[...] = jnp.zeros_like(acc_out)
        grad_b[...] = jnp.zeros_like(grad_b)
        for core in range(2):

            @pl.when(core_index() == core)
            def _(core=core):
                out_w[:, 384 * core : 384 * core + 384] = out_a[...]
                out_w[:, 384 - 384 * core : 768 - 384 * core] = out_b[...]

    proj = dot(up[...], proj_mine[...]) + dot(up_other[...], proj_theirs[...]) + proj_b[...]
    gg = dot(g[...], out_w[...], ((1,), (1,)))
    gm[...] = (gg * proj).T
    mix = mixed[...].T
    low = (mix * proj).astype(bf16)
    gated[...] = low
    gp_low = (gg * mix).astype(bf16)
    gp[...] = gp_low
    grad_b[...] += jnp.sum(gp_low.astype(f32), axis=0, keepdims=True)
    for k, ref in enumerate((up, up_other)):
        acc[k] += dot(ref[...], gp_low, ((0,), (0,)))
    acc_out[...] += dot(low, g[...], ((0,), (0,)))

    @pl.when(step == steps - 1)
    def _():
        grad_mine[...] = acc[0].astype(bf16)
        grad_theirs[...] = acc[1].astype(bf16)
        for core in range(2):

            @pl.when(core_index() == core)
            def _(core=core):
                grad_out[...] = acc_out[:, 384 * core : 384 * core + 384].astype(bf16)
                grad_send[...] = acc_out[:, 384 - 384 * core : 768 - 384 * core].astype(bf16)


def gate(up, up_other, g, mixed, proj_mine, proj_theirs, proj_b, out_a, out_b):
    n, f = up.shape
    c, d = out_a.shape[0], g.shape[1]
    return pl.pallas_call(
        gate_kernel,
        out_shape=(
            shape((c, n), f32),
            shape((n, c), bf16),
            shape((n, c), bf16),
            shape((1, c), f32),
            shape((f, c), bf16),
            shape((f, c), bf16),
            shape((c, d // 2), bf16),
            shape((c, d // 2), bf16),
        ),
        grid=(n // TILE,),
        in_specs=[tokens_by(f), tokens_by(f), tokens_by(d), by_tokens(c)]
        + [whole_block(*v.shape) for v in (proj_mine, proj_theirs, proj_b, out_a, out_b)],
        out_specs=(by_tokens(c), tokens_by(c), tokens_by(c), whole_block(1, c))
        + (whole_block(f, c), whole_block(f, c), whole_block(c, d // 2), whole_block(c, d // 2)),
        scratch_shapes=[pltpu.VMEM((2, f, c), f32), pltpu.VMEM((c, d), f32), pltpu.VMEM((c, d), bf16)],
        compiler_params=params(),
        name="gate",
    )(up, up_other, g, mixed, proj_mine, proj_theirs, proj_b, out_a, out_b)


def contract(left, right, left_dim, right_dim):
    return lax.dot_general(left, right, (((left_dim,), (right_dim,)), ((), ())), preferred_element_type=f32)


def by_core(core, zero, one):
    return jnp.where(core == 0, zero, one)


def in_order(core, mine, other, axis):
    return by_core(core, jnp.concatenate([mine, other], axis), jnp.concatenate([other, mine], axis))


def half_of(x, which, axis):
    size = x.shape[axis] // 2
    return lax.dynamic_slice_in_dim(x, which * size, size, axis)


def per_device(
    sizes,
    tokens,
    segment,
    cotangent,
    w_up,
    w_value,
    w_proj,
    w_out,
    norm_gain,
    norm_bias,
    bias_up,
    bias_value,
    bias_proj,
    bias_out,
    log_rate,
    log_step,
    input_map,
    output_map,
    skip_gain,
):
    both = ("wide", "narrow")
    core = core_index()
    pairs = [(i, i ^ 1) for i in range(sizes["narrow"])]
    staged = sizes["wide"] == 16 and sizes["narrow"] == 2

    def swap(x):
        return lax.ppermute(x, "narrow", pairs)

    tok, width = tokens.shape
    blocks = tok // T

    def by_place(x):
        return x.reshape(blocks, T, width).transpose(1, 0, 2)

    labels = segment.reshape(blocks, T)[:, 0].astype(f32)

    def whole_chip(mine, other):
        return by_core(core, jnp.stack([mine, other], 1), jnp.stack([other, mine], 1)).reshape(2 * tok, width)

    def normalise(x):
        x = x.astype(f32)
        average = jnp.mean(x, axis=-1, keepdims=True)
        centred = x - average
        scale = lax.rsqrt(jnp.mean(centred * centred, axis=-1, keepdims=True) + 1e-05)
        return centred * scale, scale

    if staged:
        vectors = (log_step, skip_gain, bias_value, bias_proj, bias_up, norm_gain, norm_bias, bias_out, labels)
        keep, send = pack(w_up, w_value, w_proj, w_out, log_rate, input_map, output_map, *vectors)
        recv = swap(send)
        other_labels = recv[192:208, 201]
        blob = merge(keep, recv)
        idle = lambda state: state

        def own_tokens(state):
            return jnp.stack([by_place(v) for v in state])

        def other_tokens(state):
            return state, swap(state)

        def chip_tokens(state):
            mine, theirs = state
            return mine, whole_chip(mine[0], theirs[0]), whole_chip(mine[1], theirs[1])

        def chip_unit(state):
            mine, x, g = state
            return mine, normalise(x)[0], g

        work = [own_tokens, other_tokens, chip_tokens, chip_unit, idle]
        placed, ((own_x, own_g), unit_chip, g_chip) = gather_rounds(blob, work, (tokens, cotangent))
        up_w, value_w, table, proj_mine, proj_theirs, out_mine, out_theirs = placed
        proj_cross = swap(proj_theirs)
        out_cross = swap(out_theirs)
        out_w = in_order(core, out_mine, out_cross, 1)
        label_row = in_order(core, labels, other_labels, 0)[None]
        coefs = coefficients(table, label_row)
        decay3, weight3, decay_row, weight_row, skip_p, value_b, proj_b, up_b, wide, masks = coefs
    else:
        own_x, own_g = by_place(tokens), by_place(cotangent)
        other_x, other_g = swap(own_x), swap(own_g)
        unit_chip, g_chip = normalise(whole_chip(own_x, other_x))[0], whole_chip(own_g, other_g)
        other_labels = swap(labels)
        whole = lambda p: lax.all_gather(p, both, axis=0, tiled=True)
        up_w = half_of(whole(w_up), core, 1)
        value_w = half_of(whole(w_value), core, 1)
        full = whole(w_proj)
        proj_mine = half_of(half_of(full, core, 1), core, 0)
        proj_theirs = half_of(half_of(full, core, 1), 1 - core, 0)
        proj_cross = half_of(half_of(full, 1 - core, 1), core, 0)
        out_w = half_of(whole(w_out), core, 0)
        out_mine, out_cross = half_of(out_w, core, 1), half_of(out_w, 1 - core, 1)
        rate_p, in_p, out_p = (half_of(whole(p).astype(f32), core, 0) for p in (log_rate, input_map, output_map))
        step_p, skip_p, value_b, proj_b = (
            half_of(whole(p).astype(f32), core, 0)[:, None] for p in (log_step, skip_gain, bias_value, bias_proj)
        )
        proj_b = proj_b.T
        up_b = half_of(whole(bias_up).astype(f32), core, 0)[None]
        wide = jnp.stack([whole(p).astype(f32) for p in (norm_gain, norm_bias, bias_out)])

    direction = core.astype(jnp.int32).reshape(1)
    if not staged:
        rate = -jnp.exp(rate_p)
        step = jnp.exp(step_p)
        decay_log = step * rate
        decay = jnp.exp(decay_log)
        gap = (decay - 1.0) / rate
        weight = out_p * gap * in_p
        masks = block_masks(in_order(core, labels[None], other_labels[None], 0), core == 1)
        decay_row, weight_row = (v.reshape(-1, 512) for v in (decay_log, weight))
        decay3, weight3 = thirds(decay_log), thirds(weight)
    normed_low, up_pre, up_low, value_pre = enter(unit_chip, wide, up_w, up_b, value_w, value_b)
    up_other = swap(up_low)
    mixed, entering = ssm_fwd(direction, value_pre, decay3, weight3, decay_row, weight_row, skip_p, masks)
    grad_mixed, gated_low, grad_proj_low, grad_proj_b, grad_proj_mine, grad_proj_theirs, grad_out_mine, grad_out_send = gate(
        up_low, up_other, g_chip, mixed, proj_mine, proj_theirs, proj_b, out_mine, out_cross
    )

    grad_proj_other = swap(grad_proj_low)
    grad_value_low, grad_mix, grad_skip, grad_value_b = ssm_bwd(
        direction, value_pre, grad_mixed, entering, decay3, weight3, decay_row, skip_p, masks
    )
    grad_up_act = contract(grad_proj_low, proj_mine, 1, 1) + contract(grad_proj_other, proj_cross, 1, 1)
    grad_up_low = (grad_up_act * gelu_grad(up_pre)).astype(bf16)
    grad_up_b = jnp.sum(grad_up_low.astype(f32), axis=0)
    grad_up_w = contract(normed_low, grad_up_low, 0, 0).astype(bf16)
    grad_value_w = contract(normed_low, grad_value_low, 0, 1).astype(bf16)

    def own_and_theirs(x):
        x = x.reshape(T, 2, blocks, width)
        return lax.dynamic_index_in_dim(x, core, 1, False), lax.dynamic_index_in_dim(x, 1 - core, 1, False)

    def by_token(x):
        return x.transpose(1, 0, 2).reshape(tok, width)

    grad_part = contract(grad_up_low, up_w, 1, 1) + contract(grad_value_low, value_w, 0, 1)
    grad_gain = jnp.sum(grad_part * unit_chip, axis=0)
    grad_shift = jnp.sum(grad_part, axis=0)
    own_gf = own_g.astype(f32)
    grad_out_b = jnp.sum(own_gf, axis=(0, 1))

    def split_parts(state):
        gated, part = state
        mine, theirs = zip(own_and_theirs(contract(gated, out_w, 1, 0)), own_and_theirs(part))
        return mine, jnp.stack([t.astype(bf16) for t in theirs])

    def exchange_parts(state):
        return state[0], swap(state[1])

    def finish_result(state):
        mine, came = state
        return by_token((own_x.astype(f32) + mine[0] + came[0] + wide[2]).astype(bf16)), mine[1] + came[1]

    def finish_tokens(state):
        result, grad_normed = state
        unit, scale = normalise(own_x)
        h = grad_normed * wide[0]
        inner = h - jnp.mean(h, axis=-1, keepdims=True) - unit * jnp.mean(h * unit, axis=-1, keepdims=True)
        return result, by_token(own_gf + inner * scale)

    if staged:
        vectors = (grad_skip, grad_value_b, grad_proj_b, grad_up_b, grad_gain, grad_shift, grad_out_b)
        small = small_sums(table, grad_mix, *vectors)
        grad_out_cross = swap(grad_out_send)
        work = [split_parts, exchange_parts, finish_result, finish_tokens, idle]
        grads = (grad_proj_mine, grad_proj_theirs, grad_out_mine, grad_out_cross, grad_up_w, grad_value_w, small)
        (mine, send), (result, grad_tokens) = scatter_all(*grads, work, (gated_low, grad_part))
        sum_proj_w, sum_out_w, sum_up_w, sum_value_w, sum_rate, sum_in, sum_out, *vectors = unpack(mine, swap(send))
        sum_step, sum_skip, sum_value_b, sum_proj_b, sum_up_b, sum_gain, sum_shift, sum_out_b = vectors
    else:

        grad_mix = grad_mix.T
        grad_weight, grad_decay = grad_mix[:, :64], grad_mix[:, 64:]
        product = out_p * in_p
        grad_ssm = (
            grad_decay * decay_log + grad_weight * (product * (decay * step - gap)),
            grad_weight * out_p * gap,
            grad_weight * in_p * gap,
            jnp.sum(grad_decay * decay_log + grad_weight * (product * decay * step), axis=1, keepdims=True),
        )

        def share(x):
            return lax.psum_scatter(x.astype(f32), both, scatter_dimension=0, tiled=True)

        def halves(x, axis):
            zero = jnp.zeros_like(x)
            return share(in_order(core, x, zero, axis))

        result, grad_tokens = finish_tokens(finish_result(exchange_parts(split_parts((gated_low, grad_part)))))
        sum_up_w, sum_value_w = halves(grad_up_w, 1), halves(grad_value_w, 1)
        sum_proj_w = halves(in_order(core, grad_proj_mine, grad_proj_theirs, 0), 1)
        sum_out_w = halves(in_order(core, grad_out_mine, grad_out_send, 1), 0)
        sum_rate, sum_in, sum_out, sum_step = (halves(v, 0) for v in grad_ssm)
        sum_step = sum_step[:, 0]
        sum_skip, sum_value_b, sum_proj_b = (halves(v, 0) for v in (grad_skip[:, 0], grad_value_b[:, 0], grad_proj_b[0]))
        sum_up_b = halves(grad_up_b, 0)
        sum_gain, sum_shift, sum_out_b = share(grad_gain), share(grad_shift), share(grad_out_b)

    return (
        result,
        grad_tokens,
        sum_up_w,
        sum_value_w,
        sum_proj_w,
        sum_out_w,
        sum_gain,
        sum_shift,
        sum_up_b,
        sum_value_b,
        sum_proj_b,
        sum_out_b,
        sum_rate,
        sum_step,
        sum_in,
        sum_out,
        sum_skip,
    )


def solution(mesh):
    rows, vector = P(("wide", "narrow"), None), P(("wide", "narrow"))
    sizes = dict(mesh.shape)
    return jax.shard_map(
        functools.partial(per_device, sizes),
        mesh=mesh,
        in_specs=(rows, vector, rows, rows, rows, rows, rows) + (vector,) * 6 + (rows, vector, rows, rows, vector),
        out_specs=(rows,) * 6 + (vector,) * 6 + (rows, vector, rows, rows, vector),
        check_vma=False,
    )
```
